32 devices in a mesh: tile: 16 (over z, y, x), chan: 2 (over core).
Axes of the slice: x: 2, y: 2, z: 4, core: 2. Of those that a mesh axis runs over, the one named last changes fastest.
Arguments:
- visibility: bfloat16 [4, 2, 131072], P('chan', None, 'tile'), may hold values from -5 to 5
- u_kernel: bfloat16 [4, 8, 131072], P('chan', None, 'tile'), may hold values from 0.099609375 to 1
- v_kernel: bfloat16 [4, 8, 131072], P('chan', None, 'tile'), may hold values from 0.099609375 to 1
- u_offset: int32 [131072], P('tile'), may hold values from 0 to 120
- v_offset: int32 [131072], P('tile'), may hold values from 0 to 120
- tile_route: int32 [512, 1], P('tile'), may hold values from 0 to 15; in each aligned block of 32 rows (0 to 31, 32 to 63, ...) at most 8 rows name the same one
- tile_slot: int32 [512], P('tile'), may hold values from 0 to 7
Outputs:
- image: float32 [1024, 1024], P(('tile', 'chan'))
The draws below stay inside these ranges and needn't reach their ends.
Inputs may be any that keep to these rules, and one draw needn't show every extreme that they name: `tile_route`: in the 32 blocks of one device at most 8 name the same owner, a bound that some block reaches of them.
All inputs are finite; a program needn't handle non-finite values.
Results may differ from the reference program's by a relative error of at most 0.0021.
The reference program's roundings to bfloat16 on the way count: a program that leaves them out, or rounds other values in their place, can miss the bound.
Values may be sent and summed in bfloat16 or wider, within the bound.
No kernel may reach another device: no remote copies, remote signals or barrier semaphores. Data moves between devices by JAX's collectives and lax.ppermute only.
A program may use at most 64 MiB of HBM per device.

```python
import math
import jax
import jax.numpy as jnp
import numpy as np
from jax import lax

NG = 16384
CH = 4
KS = 8
BLOCK = 256
TS = 128
TPD = 8
NB = 32
IMX = 1024
IMY = 1024
CPG = 2
CAP = 8
NBLOCKS = 512
VROWS = 131072
U = 2048
V = 1024
N_TILE = 16
N_CHAN = 2


def offsets_along_u(key):
    return jax.random.randint(jax.random.fold_in(key, 101), (VROWS,), 0, TS - KS + 1, dtype=jnp.int32)


def draw_u_offset(key, part):
    return offsets_along_u(key)


def draw_visibility(key, part):
    random_key = jax.random.fold_in(key, 202)
    random_part = jax.random.normal(random_key, (CH, 2, VROWS), jnp.float32)
    starts = offsets_along_u(key)
    source_pixel = IMX // 2 + NG // TS
    phase_turns = jnp.mod(starts * source_pixel, NG).astype(jnp.float32) * (2.0 * math.pi / NG)
    source = jnp.stack([jnp.cos(phase_turns), -jnp.sin(phase_turns)])[None] * 0.15
    return jnp.clip(random_part + source, -5.0, 5.0).astype(jnp.bfloat16)


def set_ends(result, own_key, smallest, top_value):
    spot = [jax.random.randint(jax.random.fold_in(own_key, axis), (), 0, length) for axis, length in enumerate(result.shape)]
    main_axis = result.shape.index(max(result.shape))
    neighbour = spot[:main_axis] + [(spot[main_axis] + 1) % result.shape[main_axis]] + spot[main_axis + 1:]
    return result.at[tuple(spot)].set(smallest).at[tuple(neighbour)].set(top_value)


def steps_of(rng, dims, split, least, top_value):
    factor_of, own = 1.0, jax.random.fold_in(rng, 6)
    for position, shards_of in split:
        steps = jnp.exp(jax.random.uniform(jax.random.fold_in(own, position), (shards_of,), jnp.float32, least / len(split), top_value / len(split)))
        factor_of = factor_of * jnp.repeat(steps, dims[position] // shards_of).reshape([-1 if axis == position else 1 for axis in range(len(dims))])
    return factor_of


def routed_block(own_key, own, number, rows, amount, top, reach, slope):
    order = jax.random.permutation(own_key, amount)
    packed, ordinary = shares(amount, rows * top, reach, slope, True), shares(amount, rows * top, reach, slope, False)
    places = jnp.arange(amount)

    def named(sizes, turn):
        used = int((sizes > 0).sum())
        fixed = max(1, used // 4)
        moved = fixed + (places - fixed + turn * (used - fixed)) % max(1, amount - fixed)
        return jnp.zeros((amount,), jnp.int32).at[order[jnp.where(places < fixed, places, moved)]].set(jnp.asarray(sizes, jnp.int32))

    sizes = jnp.where(number % 4 == 0, named(packed, number // 4), named(ordinary, number - number // 4 - 1))
    mixed = jax.random.permutation(jax.random.fold_in(own, 3), amount)
    donor, receiver = mixed[0:amount // 2 * 2:2], mixed[1:amount // 2 * 2:2]
    slack = jnp.minimum(sizes[donor] - 1, reach - sizes[receiver]) // 2
    slack = jnp.where((donor == order[0]) | (receiver == order[0]) | (sizes[receiver] == 0), 0, jnp.maximum(slack, 0))
    moved = jax.random.randint(jax.random.fold_in(own, 4), (amount // 2,), 0, 1 << 20) % (slack + 1)
    sizes = sizes.at[donor].add(-moved).at[receiver].add(moved)
    members = jnp.searchsorted(jnp.cumsum(sizes), jnp.arange(rows * top), side="right").astype(jnp.int32)
    table = members.reshape(top, rows).T
    table = table[jax.random.permutation(jax.random.fold_in(own, 1), rows)]
    turn = jax.random.randint(jax.random.fold_in(own, 2), (rows, 1), 0, top)
    return jnp.take_along_axis(table, (jnp.arange(top)[None, :] + turn) % top, axis=1)


def shares(count, total, reach, lean, full):
    weights = [(1 << 20) // math.isqrt(grade ** lean) + 1 for grade in range(1, count + 1)]
    largest = reach if full else min(reach, max(-(-total // count), total * weights[0] // sum(weights)))
    least = 1 if total - largest >= count - 1 else 0
    holding, rest = [largest] + [least] * (count - 1), total - largest - least * (count - 1)
    while rest > 0:
        free = [i for i in range(1, count) if holding[i] < largest] or [i for i in range(1, count) if holding[i] < reach]
        whole, budget = sum([weights[i] for i in free]), rest
        for i in free:
            extra = min(reach - holding[i], max(1, budget * weights[i] // whole), rest)
            holding[i] = holding[i] + extra
            rest = rest - extra
    return np.array(holding)


def setup_inputs(seed: int = 0) -> dict:
    streams_of = jax.random.split(jax.random.key(seed), 8)
    visibility = draw_visibility(jax.random.fold_in(streams_of[7], 71), 0)
    u_kernel = jnp.clip(0.099609375 + 0.9003906 * jax.random.uniform(streams_of[1], (CH, KS, VROWS), jnp.float32) ** steps_of(streams_of[1], (CH, KS, VROWS), ((0, 2), (2, 16)), -0.2, 0.2), 0.099609375, 1.0).astype(jnp.bfloat16)
    v_kernel = jnp.clip(0.099609375 + 0.9003906 * jax.random.uniform(streams_of[2], (CH, KS, VROWS), jnp.float32) ** steps_of(streams_of[2], (CH, KS, VROWS), ((0, 2), (2, 16)), -0.2, 0.2), 0.099609375, 1.0).astype(jnp.bfloat16)
    u_offset = draw_u_offset(jax.random.fold_in(streams_of[7], 71), 0)
    v_offset = set_ends(jax.random.randint(streams_of[4], (VROWS,), 0, TS - KS + 1), jax.random.fold_in(streams_of[4], 1), 0, TS - KS).astype(jnp.int32)
    tile_route_keys = jax.random.split(jax.random.fold_in(streams_of[5], 1), NBLOCKS // NB)
    tile_route_turns = jax.random.permutation(jax.random.fold_in(streams_of[5], 3), NBLOCKS // NB)
    tile_route = jax.vmap(lambda own, number: routed_block(jax.random.fold_in(streams_of[5], 2), own, number, NB, N_TILE, 1, CAP, 2))(tile_route_keys, tile_route_turns).reshape((NBLOCKS, 1))
    tile_slot = set_ends(jax.random.randint(streams_of[6], (NBLOCKS,), 0, TPD), jax.random.fold_in(streams_of[6], 1), 0, TPD - 1).astype(jnp.int32)
    return dict(visibility=visibility, u_kernel=u_kernel, v_kernel=v_kernel, u_offset=u_offset, v_offset=v_offset, tile_route=tile_route, tile_slot=tile_slot)


def phase_tables(rows_coord, cols_coord):
    phase_turns = jnp.mod(rows_coord[:, None] * cols_coord[None, :], NG)
    angles = phase_turns.astype(jnp.float32) * (2.0 * math.pi / NG)
    return (jnp.cos(angles).astype(jnp.bfloat16), jnp.sin(angles).astype(jnp.bfloat16))

def block_weights(vis_block, u_block, v_block, u_first, v_first):
    cell_index = jnp.arange(TS, dtype=jnp.int32)
    spread = jnp.arange(KS, dtype=jnp.int32)
    u_hit = u_first[None, :, None] + spread[:, None, None] == cell_index[None, None, :]
    v_hit = v_first[None, :, None] + spread[:, None, None] == cell_index[None, None, :]
    u_weight = lax.optimization_barrier(jnp.sum(jnp.where(u_hit[None], u_block[:, :, :, None].astype(jnp.float32), 0.0), axis=1))
    v_weight = lax.optimization_barrier(jnp.sum(jnp.where(v_hit[None], v_block[:, :, :, None].astype(jnp.float32), 0.0), axis=1))
    weighted = jnp.swapaxes(vis_block, 1, 2).astype(jnp.float32)[:, :, :, None] * u_weight[:, :, None, :]
    return (v_weight.astype(jnp.bfloat16), weighted.astype(jnp.bfloat16))

def reference(visibility, u_kernel, v_kernel, u_offset, v_offset, tile_route, tile_slot):
    vis_blocks = jnp.moveaxis(visibility.reshape(CH, 2, NBLOCKS, BLOCK), 2, 0)
    u_blocks = jnp.moveaxis(u_kernel.reshape(CH, KS, NBLOCKS, BLOCK), 2, 0)
    v_blocks = jnp.moveaxis(v_kernel.reshape(CH, KS, NBLOCKS, BLOCK), 2, 0)
    u_starts = u_offset.reshape(NBLOCKS, BLOCK)
    v_starts = v_offset.reshape(NBLOCKS, BLOCK)
    owners = tile_route[:, 0]
    batch = 8
    uv_grid = jnp.zeros((TPD, N_TILE, N_CHAN, TS, 2, TS), jnp.float32)

    def add_blocks(carried, turn_index):
        first_block = turn_index * batch

        def take(array):
            return lax.dynamic_slice_in_dim(array, first_block, batch, 0)
        v_weight, weighted = jax.vmap(block_weights)(take(vis_blocks), take(u_blocks), take(v_blocks), take(u_starts), take(v_starts))
        v_weight = v_weight.astype(jnp.float32).reshape(batch, N_CHAN, CPG, BLOCK, TS)
        weighted = weighted.astype(jnp.float32).reshape(batch, N_CHAN, CPG, BLOCK, 2, TS)
        tiles = jnp.einsum('bgckv,bgckpu->bgvpu', v_weight, weighted, precision=lax.Precision.HIGHEST)
        return (carried.at[take(tile_slot), take(owners)].add(tiles), None)
    uv_grid = lax.scan(add_blocks, uv_grid, jnp.arange(NBLOCKS // batch, dtype=jnp.int32))[0]
    grids = jnp.transpose(uv_grid, (2, 0, 3, 4, 1, 5)).reshape(N_CHAN, V, 2, U).astype(jnp.bfloat16)
    y_coord = jnp.arange(IMY, dtype=jnp.int32) - IMY // 2
    x_coord = jnp.arange(IMX, dtype=jnp.int32) - IMX // 2
    cos_v, sin_v = phase_tables(y_coord, jnp.arange(V, dtype=jnp.int32))
    cos_u, sin_u = phase_tables(jnp.arange(U, dtype=jnp.int32), x_coord)
    image = jnp.zeros((IMY, IMX), jnp.float32)
    for group_index in range(N_CHAN):
        flat = grids[group_index].reshape(V, 2 * U).astype(jnp.float32)
        cos_part = jnp.dot(cos_v.astype(jnp.float32), flat, precision=lax.Precision.HIGHEST).reshape(IMY, 2, U)
        sin_part = jnp.dot(sin_v.astype(jnp.float32), flat, precision=lax.Precision.HIGHEST).reshape(IMY, 2, U)
        real_part = (cos_part[:, 0] - sin_part[:, 1]).astype(jnp.bfloat16)
        imag_part = (cos_part[:, 1] + sin_part[:, 0]).astype(jnp.bfloat16)
        image = image + jnp.dot(real_part.astype(jnp.float32), cos_u.astype(jnp.float32), precision=lax.Precision.HIGHEST)
        image = image - jnp.dot(imag_part.astype(jnp.float32), sin_u.astype(jnp.float32), precision=lax.Precision.HIGHEST)
    return image / (KS * KS * math.sqrt(VROWS * CH))
```

```python
import functools
import math

import jax
import jax.numpy as jnp
import ml_dtypes
import numpy as np
from jax import lax
from jax.experimental import pallas as pl
from jax.experimental.pallas import tpu as pltpu
from jax.sharding import PartitionSpec as P

NG = 16384
CH = 4
KS = 8
BLOCK = 256
TS = 128
TPD = 8
NB = 32
IMX = 1024
IMY = 1024
ROWS = 80


def phase_table(rows_coord, cols_coord):
    turns = np.mod(rows_coord[:, None].astype(np.int64) * cols_coord[None, :].astype(np.int64), NG)
    angles = turns.astype(np.float64) * (2.0 * math.pi / NG)
    return np.cos(angles).astype(ml_dtypes.bfloat16), np.sin(angles).astype(ml_dtypes.bfloat16)


def column_table():
    cos_v, sin_v = phase_table(np.arange(IMY) - IMY // 2, np.arange(TPD * TS))
    return np.concatenate([cos_v, sin_v], axis=1)


def image_table(bands):
    cos_u, sin_u = phase_table(np.arange(bands * TS), np.arange(IMX) - IMX // 2)
    both = np.stack([cos_u.reshape(bands, TS, IMX), (-sin_u).reshape(bands, TS, IMX)], axis=1)
    return both.reshape(bands * 2 * TS, IMX)


def pack_kernel(capacity, route, slot, u_ref, v_ref, vis_ref, uo_ref, vo_ref, out_ref, count):
    owners = out_ref.shape[0] // capacity
    out_ref[...] = jnp.zeros_like(out_ref)

    def clear(owner, _):
        count[owner] = 0
        return 0

    lax.fori_loop(0, owners, clear, 0)
    for block in range(NB):
        owner = route[block]
        rank = count[owner]
        count[owner] = rank + 1
        target = owner * capacity + rank
        place = jnp.full((1, TS), slot[block] + 1, jnp.int32).astype(jnp.float32)
        misc = []
        for half in range(2):
            lanes = slice(block * BLOCK + half * TS, block * BLOCK + half * TS + TS)
            row = block * 2 + half
            out_ref[target, 16 * half:16 * half + 16, :] = u_ref[:, lanes]
            out_ref[target, 32 + 16 * half:48 + 16 * half, :] = v_ref[:, lanes]
            misc += [
                vis_ref[0, :, lanes].astype(jnp.float32),
                vis_ref[1, :, lanes].astype(jnp.float32),
                uo_ref[row:row + 1, :].astype(jnp.float32),
                vo_ref[row:row + 1, :].astype(jnp.float32),
                place,
                jnp.zeros((1, TS), jnp.float32),
            ]
        out_ref[target, 64:80, :] = jnp.concatenate(misc, axis=0).astype(jnp.bfloat16)


def turned(kernel, first):
    for bit in (1, 2, 4):
        kernel = jnp.where((first & bit) != 0, pltpu.roll(kernel, bit, 0), kernel)
    return kernel


def spread(kernel, first_tile):
    both = jnp.concatenate([kernel, kernel], axis=0).astype(jnp.bfloat16)
    zero = jnp.zeros_like(both)
    return jnp.concatenate(
        [jnp.where(first_tile == pair * 2, both, zero) for pair in range(TS // 16)], axis=0
    )


def tile_of(first):
    sub = lax.broadcasted_iota(jnp.int32, (8, TS), 0)
    tile = lax.shift_right_logical(first + ((sub - first) & 7), 3)
    return jnp.concatenate([tile, tile - 1], axis=0).astype(jnp.float32).astype(jnp.bfloat16)


def block_tile(got_ref, index):
    v_parts, w_parts = [], []
    misc = got_ref[index, 64:80, :].astype(jnp.float32)
    for half in range(2):
        u_two = got_ref[index, 16 * half:16 * half + 16, :].astype(jnp.float32)
        v_two = got_ref[index, 32 + 16 * half:48 + 16 * half, :].astype(jnp.float32)
        own = misc[8 * half:8 * half + 8]
        u_first = jnp.broadcast_to(own[4:5], (8, TS)).astype(jnp.int32)
        v_first = jnp.broadcast_to(own[5:6], (8, TS)).astype(jnp.int32)
        u_tile, v_tile = tile_of(u_first), tile_of(v_first)
        for chan in range(2):
            v_parts.append(spread(turned(v_two[8 * chan:8 * chan + 8], v_first), v_tile))
            u_turned = turned(u_two[8 * chan:8 * chan + 8], u_first)
            w_parts.append(jnp.concatenate(
                [spread(u_turned * own[2 * chan + part:2 * chan + part + 1], u_tile) for part in range(2)],
                axis=0,
            ))
    v_all = jnp.concatenate(v_parts, axis=1)
    w_all = jnp.concatenate(w_parts, axis=1)
    return lax.dot_general(v_all, w_all, (((1,), (1,)), ((), ())), preferred_element_type=jnp.float32)


def grid_kernel(places, got_ref, table_hbm, out_ref, grid, table, order, sem):
    copy = pltpu.make_async_copy(table_hbm, table, sem)
    copy.start()
    grid[...] = jnp.zeros_like(grid)
    slots = got_ref.shape[0]

    def list_slot(index, carried):
        filled, spare = carried
        taken = places[index] > 0

        @pl.when(taken)
        def _():
            order[filled] = index

        return filled + taken.astype(jnp.int32), jnp.where(taken, spare, index)

    filled, spare = lax.fori_loop(0, slots, list_slot, (jnp.int32(0), jnp.int32(0)))
    order[filled] = spare

    def add_pair(turn, _):
        for lane in range(2):
            index = order[turn * 2 + lane]
            place = jnp.maximum(places[index] - 1, 0)
            rows = pl.ds(pl.multiple_of(place * TS, TS), TS)
            grid[rows, :] += block_tile(got_ref, index)
        return 0

    lax.fori_loop(0, (filled + 1) // 2, add_pair, 0)
    copy.wait()
    rounded = grid[...].astype(jnp.bfloat16)
    real, imag = rounded[:, :TS], rounded[:, TS:]
    both = jnp.concatenate([rounded, jnp.concatenate([-imag, real], axis=1)], axis=0)
    step = 256
    for first in range(0, IMY, step):
        out_ref[first:first + step, :] = jnp.dot(
            table[first:first + step, :], both, preferred_element_type=jnp.float32
        ).astype(jnp.bfloat16)


def image_kernel(scale, got_ref, table_ref, out_ref, total):
    turn = pl.program_id(0)

    @pl.when(turn == 0)
    def _():
        total[...] = jnp.zeros_like(total)

    rows = got_ref.shape[2]
    part = total[...]
    for band in range(got_ref.shape[0]):
        both = jnp.concatenate([got_ref[band, 0], got_ref[band, 1]], axis=0)
        part = part + jnp.dot(
            both, table_ref[band * 2 * TS:(band + 1) * 2 * TS, :], preferred_element_type=jnp.float32
        )
    total[...] = part

    @pl.when(turn == pl.num_programs(0) - 1)
    def _():
        out_ref[...] = (part[:rows] + part[rows:]) * scale


VMEM = pl.BlockSpec(memory_space=pltpu.VMEM)
SMEM = pl.BlockSpec(memory_space=pltpu.SMEM)
PARAMS = pltpu.CompilerParams(vmem_limit_bytes=48 * 1024 * 1024)


def body(visibility, u_kernel, v_kernel, u_offset, v_offset, tile_route, tile_slot):
    bands = lax.axis_size("tile")
    groups = lax.axis_size("chan")
    local_rows = visibility.shape[2]
    capacity = 4 * NB // bands
    slots = bands * capacity
    packed = pl.pallas_call(
        functools.partial(pack_kernel, capacity),
        out_shape=jax.ShapeDtypeStruct((slots, ROWS, TS), jnp.bfloat16),
        in_specs=[SMEM, SMEM, VMEM, VMEM, VMEM, VMEM, VMEM],
        out_specs=VMEM,
        scratch_shapes=[pltpu.SMEM((bands,), jnp.int32)],
        compiler_params=PARAMS,
    )(
        tile_route[:, 0],
        tile_slot,
        u_kernel.reshape(2 * KS, local_rows),
        v_kernel.reshape(2 * KS, local_rows),
        visibility,
        u_offset.reshape(NB * 2, TS),
        v_offset.reshape(NB * 2, TS),
    )
    got = lax.all_to_all(packed, "tile", split_axis=0, concat_axis=0, tiled=True)
    places = got[:, 70, 0].astype(jnp.int32)
    columns = pl.pallas_call(
        grid_kernel,
        out_shape=jax.ShapeDtypeStruct((IMY, 2 * TS), jnp.bfloat16),
        in_specs=[SMEM, VMEM, pl.BlockSpec(memory_space=pl.ANY)],
        out_specs=VMEM,
        scratch_shapes=[
            pltpu.VMEM((TPD * TS, 2 * TS), jnp.float32),
            pltpu.VMEM((IMY, 2 * TPD * TS), jnp.bfloat16),
            pltpu.SMEM((slots + 8,), jnp.int32),
            pltpu.SemaphoreType.DMA,
        ],
        compiler_params=PARAMS,
    )(places, got, jnp.asarray(column_table()))
    rows_y = IMY // (bands * groups)
    sent = lax.all_to_all(
        columns.reshape(bands * groups, rows_y, 2 * TS), ("tile", "chan"), split_axis=0, concat_axis=0, tiled=True
    )
    per_turn = 4
    scale = 1.0 / (KS * KS * math.sqrt(local_rows * bands * CH))
    return pl.pallas_call(
        functools.partial(image_kernel, scale),
        out_shape=jax.ShapeDtypeStruct((rows_y, IMX), jnp.float32),
        grid=(bands // per_turn,),
        in_specs=[
            pl.BlockSpec((per_turn, groups, rows_y, 2 * TS), lambda turn: (turn, 0, 0, 0)),
            pl.BlockSpec((per_turn * 2 * TS, IMX), lambda turn: (turn, 0)),
        ],
        out_specs=pl.BlockSpec((rows_y, IMX), lambda turn: (0, 0)),
        scratch_shapes=[pltpu.VMEM((groups * rows_y, IMX), jnp.float32)],
        compiler_params=PARAMS,
    )(sent.reshape(bands, groups, rows_y, 2 * TS), jnp.asarray(image_table(bands)))


def solution(mesh):
    placed = (
        P("chan", None, "tile"),
        P("chan", None, "tile"),
        P("chan", None, "tile"),
        P("tile"),
        P("tile"),
        P("tile", None),
        P("tile"),
    )
    return jax.shard_map(
        body, mesh=mesh, in_specs=placed, out_specs=P(("tile", "chan"), None), check_vma=False
    )
```

```python
import functools
import math

import jax
import jax.numpy as jnp
import ml_dtypes
import numpy as np
from jax import lax
from jax.experimental import pallas as pl
from jax.experimental.pallas import tpu as pltpu
from jax.sharding import PartitionSpec as P

NG = 16384
CH = 4
KS = 8
BLOCK = 256
TS = 128
TPD = 8
NB = 32
IMX = 1024
IMY = 1024
ROWS = 80
TILES = ROWS // 16
DIRECT = 2
MANY = 255


def phase_table(rows_coord, cols_coord):
    turns = np.mod(rows_coord[:, None].astype(np.int64) * cols_coord[None, :].astype(np.int64), NG)
    angles = turns.astype(np.float64) * (2.0 * math.pi / NG)
    return np.cos(angles).astype(ml_dtypes.bfloat16), np.sin(angles).astype(ml_dtypes.bfloat16)


def column_table():
    cos_v, sin_v = phase_table(np.arange(IMY) - IMY // 2, np.arange(TPD * TS))
    return np.concatenate([cos_v, sin_v], axis=1)


def image_table(bands):
    cos_u, sin_u = phase_table(np.arange(bands * TS), np.arange(IMX) - IMX // 2)
    both = np.stack([cos_u.reshape(bands, TS, IMX), (-sin_u).reshape(bands, TS, IMX)], axis=1)
    return both


def shared_table(both):
    bands = both.shape[0]
    cut = both.reshape(bands, 2, bands, TS // bands, IMX)
    return np.swapaxes(cut, 1, 2).reshape(bands * 2 * TS, IMX)


def full_pack_kernel(capacity, route, slot, u_ref, v_ref, vis_ref, uo_ref, vo_ref, out_ref, count):
    owners = out_ref.shape[0] // (capacity * TILES)
    out_ref[...] = jnp.zeros_like(out_ref)

    def clear(owner, _):
        count[owner] = 0
        return 0

    lax.fori_loop(0, owners, clear, 0)
    for block in range(NB):
        owner = route[block]
        rank = count[owner]
        count[owner] = rank + 1
        base = (owner * capacity + rank) * TILES
        place = jnp.full((1, TS), slot[block] + 1, jnp.int32).astype(jnp.float32)
        misc = []
        for half in range(2):
            lanes = slice(block * BLOCK + half * TS, block * BLOCK + half * TS + TS)
            row = block * 2 + half
            out_ref[base + half] = u_ref[:, lanes]
            out_ref[base + 2 + half] = v_ref[:, lanes]
            misc += [
                vis_ref[0, :, lanes].astype(jnp.float32),
                vis_ref[1, :, lanes].astype(jnp.float32),
                uo_ref[row:row + 1, :].astype(jnp.float32),
                vo_ref[row:row + 1, :].astype(jnp.float32),
                place,
                jnp.zeros((1, TS), jnp.float32),
            ]
        out_ref[base + 4] = jnp.concatenate(misc, axis=0).astype(jnp.bfloat16)


def turned(kernel, first):
    for bit in (1, 2, 4):
        kernel = jnp.where((first & bit) != 0, pltpu.roll(kernel, bit, 0), kernel)
    return kernel


def spread(kernel, first_tile):
    both = jnp.concatenate([kernel, kernel], axis=0).astype(jnp.bfloat16)
    zero = jnp.zeros_like(both)
    return jnp.concatenate(
        [jnp.where(first_tile == pair * 2, both, zero) for pair in range(TS // 16)], axis=0
    )


def tile_of(first, twice):
    sub = lax.broadcasted_iota(jnp.int32, (8, TS), 0)
    tile = lax.shift_right_logical(first + ((sub - first) & 7), 3)
    return jnp.concatenate([tile, tile if twice else tile - 1], axis=0).astype(jnp.float32).astype(jnp.bfloat16)


def spread_pair(first, second, first_tile):
    both = jnp.concatenate([first, second], axis=0).astype(jnp.bfloat16)
    zero = jnp.zeros_like(both)
    return jnp.concatenate([jnp.where(first_tile == tile, both, zero) for tile in range(TS // 8)], axis=0)


def block_factors(halves, shared):
    v_parts, w_parts = [], []
    for u_two, v_two, own in halves:
        u_first = jnp.broadcast_to(own[4:5], (8, TS)).astype(jnp.int32)
        v_first = jnp.broadcast_to(own[5:6], (8, TS)).astype(jnp.int32)
        u_tile, v_tile = tile_of(u_first, shared), tile_of(v_first, False)
        for chan in range(2):
            v_parts.append(spread(turned(v_two[8 * chan:8 * chan + 8], v_first), v_tile))
            u_turned = turned(u_two[8 * chan:8 * chan + 8], u_first)
            real, imag = [u_turned * own[2 * chan + part:2 * chan + part + 1] for part in range(2)]
            if shared:
                w_parts.append(spread_pair(real, imag, u_tile))
            else:
                w_parts.append(jnp.concatenate([spread(real, u_tile), spread(imag, u_tile)], axis=0))
    return jnp.concatenate(v_parts, axis=1), jnp.concatenate(w_parts, axis=1)


def dot_rows(left, right):
    return lax.dot_general(left, right, (((1,), (1,)), ((), ())), preferred_element_type=jnp.float32)


def pack_kernel(
    bands, shared,
    route_hbm, slot_hbm, u_hbm, v_hbm, vis_hbm, uo_hbm, vo_hbm, out_ref,
    route, slot, u_ref, v_ref, vis_ref, uo_ref, vo_ref, count, listed, grid, sems,
):
    pairs = (
        (route_hbm, route), (slot_hbm, slot), (u_hbm, u_ref), (v_hbm, v_ref),
        (vis_hbm, vis_ref), (uo_hbm, uo_ref), (vo_hbm, vo_ref),
    )
    copies = [pltpu.make_async_copy(source, target, sems.at[turn]) for turn, (source, target) in enumerate(pairs)]
    for copy in copies:
        copy.start()
    per_owner = out_ref.shape[0] // bands

    def clear(owner, _):
        count[owner] = 0
        return 0

    lax.fori_loop(0, bands, clear, 0)
    if shared:
        grid[...] = jnp.zeros_like(grid)
    copies[0].wait()
    copies[1].wait()

    mark = jnp.int32(0)
    if shared:
        for block in range(NB):
            owner = route[block]
            seen = count[owner]
            count[owner] = seen + 1
            mark = jnp.where(seen == DIRECT, jnp.where(mark == 0, owner + 1, MANY), mark)
        lax.fori_loop(0, bands, clear, 0)
    marks = jnp.broadcast_to(mark, (1, TS)).astype(jnp.float32)
    nothing = jnp.zeros((7, TS), jnp.float32)
    blank = jnp.concatenate([nothing, marks, nothing, marks], axis=0).astype(jnp.bfloat16)
    empty = jnp.zeros((16, TS), jnp.bfloat16)
    for owner in range(bands):
        for rank in range(DIRECT):
            base = owner * per_owner + rank * TILES
            for tile in range(TILES - 1):
                out_ref[base + tile] = empty
            out_ref[base + TILES - 1] = blank
    for copy in copies[2:]:
        copy.wait()

    filled = jnp.int32(0)
    for block in range(NB):
        owner = route[block]
        rank = count[owner]
        count[owner] = rank + 1
        apart = (owner + 1 == mark) | (rank >= DIRECT)
        base = owner * per_owner + rank * TILES
        if shared:
            listed[filled] = block
            filled = filled + apart.astype(jnp.int32)

        @pl.when(jnp.logical_not(apart))
        def _():
            place = jnp.full((1, TS), slot[block] + 1, jnp.int32).astype(jnp.float32)
            misc = []
            for half in range(2):
                lanes = slice(block * BLOCK + half * TS, block * BLOCK + half * TS + TS)
                row = block * 2 + half
                out_ref[base + half] = u_ref[:, lanes]
                out_ref[base + 2 + half] = v_ref[:, lanes]
                misc += [
                    vis_ref[0, :, lanes].astype(jnp.float32),
                    vis_ref[1, :, lanes].astype(jnp.float32),
                    uo_ref[row:row + 1, :].astype(jnp.float32),
                    vo_ref[row:row + 1, :].astype(jnp.float32),
                    place,
                    marks,
                ]
            out_ref[base + 4] = jnp.concatenate(misc, axis=0).astype(jnp.bfloat16)

    if not shared:
        return

    def add_block(turn, _):
        block = listed[turn]
        halves = []
        for half in range(2):
            lanes = pl.ds(pl.multiple_of(block * BLOCK + half * TS, TS), TS)
            row = pl.ds(block * 2 + half, 1)
            own = jnp.concatenate(
                [
                    vis_ref[0, :, lanes].astype(jnp.float32),
                    vis_ref[1, :, lanes].astype(jnp.float32),
                    uo_ref[row, :].astype(jnp.float32),
                    vo_ref[row, :].astype(jnp.float32),
                ],
                axis=0,
            )
            halves.append((u_ref[:, lanes].astype(jnp.float32), v_ref[:, lanes].astype(jnp.float32), own))
        v_all, w_all = block_factors(halves, True)
        cells = pl.ds(pl.multiple_of(slot[block] * TS, TS), TS)
        grid[:, cells] += dot_rows(w_all, v_all)
        return 0

    lax.fori_loop(0, filled, add_block, 0)
    for owner in range(bands):
        for place in range(TPD):
            out_ref[owner * per_owner + DIRECT * TILES + place] = grid[
                16 * owner:16 * owner + 16, TS * place:TS * place + TS
            ].astype(jnp.bfloat16)


def got_tile(got_ref, base):
    misc = got_ref[base + 4].astype(jnp.float32)
    halves = [
        (got_ref[base + half].astype(jnp.float32), got_ref[base + 2 + half].astype(jnp.float32), misc[8 * half:8 * half + 8])
        for half in range(2)
    ]
    v_all, w_all = block_factors(halves, False)
    return misc, dot_rows(v_all, w_all)


def write_columns(grid, table, out_ref, extra):
    rounded = grid[...].astype(jnp.bfloat16)
    real, imag = rounded[:, :TS], rounded[:, TS:]
    both = jnp.concatenate([rounded, jnp.concatenate([-imag, real], axis=1)], axis=0)
    rows = IMY // out_ref.shape[0]
    step = 256
    for first in range(0, IMY, step):
        part = jnp.dot(table[first:first + step, :], both, preferred_element_type=jnp.float32)
        if extra is not None:
            more = dot_rows(extra, table[first:first + step, :])
        for row in range(0, step, rows):
            pieces = [part[row:row + rows, :TS], part[row:row + rows, TS:]]
            if extra is not None:
                lane = row // TS * TS
                pieces.append(more[:, lane:lane + TS])
            elif out_ref.shape[1] > 2 * rows:
                pieces.append(jnp.zeros((out_ref.shape[1] - 2 * rows, TS), jnp.float32))
            out_ref[(first + row) // rows] = jnp.concatenate(pieces, axis=0).astype(jnp.bfloat16)


def full_grid_kernel(places, got_ref, table_hbm, out_ref, grid, table, sem):
    copy = pltpu.make_async_copy(table_hbm, table, sem)
    copy.start()
    grid[...] = jnp.zeros_like(grid)
    tiles = got_ref.shape[0]

    def add_slot(index, _):
        @pl.when(places[index] > 0)
        def _():
            rows = pl.ds(pl.multiple_of((places[index] - 1) * TS, TS), TS)
            grid[rows, :] += got_tile(got_ref, index * TILES)[1]

        return 0

    lax.fori_loop(0, tiles // TILES, add_slot, 0)
    copy.wait()
    write_columns(grid, table, out_ref, None)


def grid_kernel(bands, shared, got_ref, table_hbm, out_ref, flags, grid, table, sem):
    copy = pltpu.make_async_copy(table_hbm, table, sem)
    copy.start()
    grid[...] = jnp.zeros_like(grid)
    per_owner = got_ref.shape[0] // bands

    def add_source(source, carried):
        least, most = carried
        for rank in range(DIRECT):
            misc, tile = got_tile(got_ref, source * per_owner + rank * TILES)
            place = jnp.maximum(misc[6, 0].astype(jnp.int32) - 1, 0)
            rows = pl.ds(pl.multiple_of(place * TS, TS), TS)
            grid[rows, :] += tile
        return jnp.minimum(least, misc[:8]), jnp.maximum(most, misc[:8])

    start = (jnp.full((8, TS), float(MANY), jnp.float32), jnp.zeros((8, TS), jnp.float32))
    least, most = lax.fori_loop(0, bands, add_source, start)
    low, high = least[7, 0].astype(jnp.int32), most[7, 0].astype(jnp.int32)
    flags[0] = ((low == high) & (high != MANY)).astype(jnp.int32)
    flags[1] = jnp.maximum(jnp.where(high == MANY, 0, high) - 1, 0)
    extra = None
    if shared:
        parts = []
        for place in range(TPD):
            total = jnp.zeros((16, TS), jnp.float32)
            for source in range(bands):
                total += got_ref[source * per_owner + DIRECT * TILES + place].astype(jnp.float32)
            parts.append(total)
        own = jnp.concatenate(parts, axis=1).astype(jnp.bfloat16).astype(jnp.float32)
        other = jnp.concatenate([-own[8:], own[:8]], axis=0)
        extra = jnp.concatenate([own, other], axis=1).astype(jnp.bfloat16)
    copy.wait()
    write_columns(grid, table, out_ref, extra)


def band_dot(got_ref, table_ref, first, rows):
    total = None
    for band in range(got_ref.shape[0]):
        both = jnp.concatenate(
            [
                jnp.concatenate([got_ref[band, group, :rows, :], got_ref[band, group, rows:2 * rows, :]], axis=1)
                for group in range(got_ref.shape[1])
            ],
            axis=0,
        )
        part = jnp.dot(
            both, table_ref[band * 2 * TS:(band + 1) * 2 * TS, :], preferred_element_type=jnp.float32
        )
        total = part if total is None else total + part
    return total


def image_kernel(scale, flags, got_ref, table_ref, shared_hbm, out_ref, shared, sem):
    rows = out_ref.shape[0]
    lines = shared.shape[0]
    copy = pltpu.make_async_copy(
        shared_hbm.at[pl.ds(pl.multiple_of(flags[1] * lines, lines), lines), :], shared, sem
    )
    copy.start()
    total = band_dot(got_ref, table_ref, 0, rows)
    image = total[:rows] + total[rows:]
    turn = (lax.axis_index("tile") * got_ref.shape[1] + lax.axis_index("chan")) % (TS // rows)
    copy.wait()
    for group in range(got_ref.shape[1]):
        left = jnp.concatenate([got_ref[band, group, 2 * rows:, :] for band in range(got_ref.shape[0])], axis=0)
        left = pltpu.roll(left.astype(jnp.float32), lax.rem(TS - turn * rows, TS), 1)[:, :rows].astype(jnp.bfloat16)
        image = image + lax.dot_general(
            left, shared[...], (((0,), (0,)), ((), ())), preferred_element_type=jnp.float32
        )
    out_ref[...] = image * scale


def plain_image_kernel(scale, got_ref, table_ref, out_ref, total):
    turn = pl.program_id(0)

    @pl.when(turn == 0)
    def _():
        total[...] = jnp.zeros_like(total)

    rows = out_ref.shape[0]
    total[...] += band_dot(got_ref, table_ref, 0, rows)

    @pl.when(turn == pl.num_programs(0) - 1)
    def _():
        out_ref[...] = (total[:rows] + total[rows:]) * scale


VMEM = pl.BlockSpec(memory_space=pltpu.VMEM)
SMEM = pl.BlockSpec(memory_space=pltpu.SMEM)
ANY = pl.BlockSpec(memory_space=pl.ANY)
PARAMS = pltpu.CompilerParams(vmem_limit_bytes=40 * 1024 * 1024)


def body(visibility, u_kernel, v_kernel, u_offset, v_offset, tile_route, tile_slot):
    bands = lax.axis_size("tile")
    groups = lax.axis_size("chan")
    local_rows = visibility.shape[2]
    capacity = 4 * NB // bands
    shared = capacity > DIRECT
    per_owner = DIRECT * TILES + (TPD if shared else 0)
    rows_y = IMY // (bands * groups)
    sent_rows = 2 * rows_y + (16 if shared else 0)
    columns_shape = jax.ShapeDtypeStruct((bands * groups, sent_rows, TS), jnp.bfloat16)
    v_table = jnp.asarray(column_table())
    both = image_table(bands)
    u_table = jnp.asarray(both.reshape(bands * 2 * TS, IMX))
    operands = (
        tile_route[:, 0],
        tile_slot,
        u_kernel.reshape(2 * KS, local_rows),
        v_kernel.reshape(2 * KS, local_rows),
        visibility,
        u_offset.reshape(NB * 2, TS),
        v_offset.reshape(NB * 2, TS),
    )
    grid_scratch = [
        pltpu.VMEM((TPD * TS, 2 * TS), jnp.float32),
        pltpu.VMEM((IMY, 2 * TPD * TS), jnp.bfloat16),
        pltpu.SemaphoreType.DMA,
    ]
    packed = pl.pallas_call(
        functools.partial(pack_kernel, bands, shared),
        out_shape=jax.ShapeDtypeStruct((bands * per_owner, 16, TS), jnp.bfloat16),
        in_specs=[ANY] * 7,
        out_specs=VMEM,
        scratch_shapes=[
            pltpu.SMEM((NB,), jnp.int32),
            pltpu.SMEM((NB,), jnp.int32),
            pltpu.VMEM((2 * KS, local_rows), jnp.bfloat16),
            pltpu.VMEM((2 * KS, local_rows), jnp.bfloat16),
            pltpu.VMEM(visibility.shape, jnp.bfloat16),
            pltpu.VMEM((NB * 2, TS), jnp.int32),
            pltpu.VMEM((NB * 2, TS), jnp.int32),
            pltpu.SMEM((bands,), jnp.int32),
            pltpu.SMEM((NB + 1,), jnp.int32),
            pltpu.VMEM((2 * TS, TPD * TS), jnp.float32),
            pltpu.SemaphoreType.DMA((7,)),
        ],
        compiler_params=PARAMS,
    )(*operands)
    got = lax.all_to_all(packed, "tile", split_axis=0, concat_axis=0, tiled=True)
    columns, flags = pl.pallas_call(
        functools.partial(grid_kernel, bands, shared),
        out_shape=(columns_shape, jax.ShapeDtypeStruct((2,), jnp.int32)),
        in_specs=[VMEM, ANY],
        out_specs=(VMEM, SMEM),
        scratch_shapes=grid_scratch,
        compiler_params=PARAMS,
    )(got, v_table)

    def every_slot(_):
        slots = bands * capacity
        packed = pl.pallas_call(
            functools.partial(full_pack_kernel, capacity),
            out_shape=jax.ShapeDtypeStruct((slots * TILES, 16, TS), jnp.bfloat16),
            in_specs=[SMEM, SMEM, VMEM, VMEM, VMEM, VMEM, VMEM],
            out_specs=VMEM,
            scratch_shapes=[pltpu.SMEM((bands,), jnp.int32)],
            compiler_params=PARAMS,
        )(*operands)
        got = lax.all_to_all(packed, "tile", split_axis=0, concat_axis=0, tiled=True)
        places = got.reshape(slots, TILES, 16, TS)[:, TILES - 1, 6, 0].astype(jnp.int32)
        return pl.pallas_call(
            full_grid_kernel,
            out_shape=columns_shape,
            in_specs=[SMEM, VMEM, ANY],
            out_specs=VMEM,
            scratch_shapes=grid_scratch,
            compiler_params=PARAMS,
        )(places, got, v_table)

    if shared:
        columns = lax.cond(flags[0] == 1, lambda kept: kept, every_slot, columns)
    sent = lax.all_to_all(columns, ("tile", "chan"), split_axis=0, concat_axis=0, tiled=True)
    sent = sent.reshape(bands, groups, sent_rows, TS)
    scale = 1.0 / (KS * KS * math.sqrt(local_rows * bands * CH))
    out_shape = jax.ShapeDtypeStruct((rows_y, IMX), jnp.float32)
    if shared:
        return pl.pallas_call(
            functools.partial(image_kernel, scale),
            out_shape=out_shape,
            in_specs=[SMEM, VMEM, VMEM, ANY],
            out_specs=VMEM,
            scratch_shapes=[pltpu.VMEM((2 * TS, IMX), jnp.bfloat16), pltpu.SemaphoreType.DMA],
            compiler_params=PARAMS,
        )(flags, sent, u_table, jnp.asarray(shared_table(both)))
    per_turn = 4
    return pl.pallas_call(
        functools.partial(plain_image_kernel, scale),
        out_shape=out_shape,
        grid=(bands // per_turn,),
        in_specs=[
            pl.BlockSpec((per_turn, groups, sent_rows, TS), lambda turn: (turn, 0, 0, 0)),
            pl.BlockSpec((per_turn * 2 * TS, IMX), lambda turn: (turn, 0)),
        ],
        out_specs=pl.BlockSpec((rows_y, IMX), lambda turn: (0, 0)),
        scratch_shapes=[pltpu.VMEM((groups * rows_y, IMX), jnp.float32)],
        compiler_params=PARAMS,
    )(sent, u_table)


def solution(mesh):
    placed = (
        P("chan", None, "tile"),
        P("chan", None, "tile"),
        P("chan", None, "tile"),
        P("tile"),
        P("tile"),
        P("tile", None),
        P("tile"),
    )
    return jax.shard_map(
        body, mesh=mesh, in_specs=placed, out_specs=P(("tile", "chan"), None), check_vma=False
    )
```

```python
import functools
import math

import jax
import jax.numpy as jnp
import ml_dtypes
import numpy as np
from jax import lax
from jax.experimental import pallas as pl
from jax.experimental.pallas import tpu as pltpu
from jax.sharding import PartitionSpec as P

NG = 16384
CH = 4
KS = 8
BLOCK = 256
TS = 128
TPD = 8
NB = 32
IMX = 1024
IMY = 1024
ROWS = 80
TILES = ROWS // 16
DIRECT = 2
PEERS = 4
MANY = 255


def phase_table(rows_coord, cols_coord):
    turns = np.mod(rows_coord[:, None].astype(np.int64) * cols_coord[None, :].astype(np.int64), NG)
    angles = turns.astype(np.float64) * (2.0 * math.pi / NG)
    return np.cos(angles).astype(ml_dtypes.bfloat16), np.sin(angles).astype(ml_dtypes.bfloat16)


def column_table():
    cos_v, sin_v = phase_table(np.arange(IMY) - IMY // 2, np.arange(TPD * TS))
    return np.concatenate([cos_v, sin_v], axis=1)


def image_table(bands):
    cos_u, sin_u = phase_table(np.arange(bands * TS), np.arange(IMX) - IMX // 2)
    both = np.stack([cos_u.reshape(bands, TS, IMX), (-sin_u).reshape(bands, TS, IMX)], axis=1)
    return both.reshape(bands * 2 * TS, IMX)


def full_pack_kernel(capacity, route, slot, u_ref, v_ref, vis_ref, uo_ref, vo_ref, out_ref, count):
    owners = out_ref.shape[0] // (capacity * TILES)
    out_ref[...] = jnp.zeros_like(out_ref)

    def clear(owner, _):
        count[owner] = 0
        return 0

    lax.fori_loop(0, owners, clear, 0)
    for block in range(NB):
        owner = route[block]
        rank = count[owner]
        count[owner] = rank + 1
        base = (owner * capacity + rank) * TILES
        place = jnp.full((1, TS), slot[block] + 1, jnp.int32).astype(jnp.float32)
        misc = []
        for half in range(2):
            lanes = slice(block * BLOCK + half * TS, block * BLOCK + half * TS + TS)
            row = block * 2 + half
            out_ref[base + half] = u_ref[:, lanes]
            out_ref[base + 2 + half] = v_ref[:, lanes]
            misc += [
                vis_ref[0, :, lanes].astype(jnp.float32),
                vis_ref[1, :, lanes].astype(jnp.float32),
                uo_ref[row:row + 1, :].astype(jnp.float32),
                vo_ref[row:row + 1, :].astype(jnp.float32),
                place,
                jnp.zeros((1, TS), jnp.float32),
            ]
        out_ref[base + 4] = jnp.concatenate(misc, axis=0).astype(jnp.bfloat16)


def turned(kernel, first):
    for bit in (1, 2, 4):
        kernel = jnp.where((first & bit) != 0, pltpu.roll(kernel, bit, 0), kernel)
    return kernel


def spread(kernel, first_tile):
    both = jnp.concatenate([kernel, kernel], axis=0).astype(jnp.bfloat16)
    zero = jnp.zeros_like(both)
    return jnp.concatenate(
        [jnp.where(first_tile == pair * 2, both, zero) for pair in range(TS // 16)], axis=0
    )


def tile_of(first):
    sub = lax.broadcasted_iota(jnp.int32, (8, TS), 0)
    tile = lax.shift_right_logical(first + ((sub - first) & 7), 3)
    return jnp.concatenate([tile, tile - 1], axis=0).astype(jnp.float32).astype(jnp.bfloat16)


def block_tile(halves):
    v_parts, w_parts = [], []
    for u_two, v_two, own in halves:
        u_first = jnp.broadcast_to(own[4:5], (8, TS)).astype(jnp.int32)
        v_first = jnp.broadcast_to(own[5:6], (8, TS)).astype(jnp.int32)
        u_tile, v_tile = tile_of(u_first), tile_of(v_first)
        for chan in range(2):
            v_parts.append(spread(turned(v_two[8 * chan:8 * chan + 8], v_first), v_tile))
            u_turned = turned(u_two[8 * chan:8 * chan + 8], u_first)
            w_parts.append(jnp.concatenate(
                [spread(u_turned * own[2 * chan + part:2 * chan + part + 1], u_tile) for part in range(2)],
                axis=0,
            ))
    return dot_rows(jnp.concatenate(w_parts, axis=1), jnp.concatenate(v_parts, axis=1))


def dot_rows(left, right):
    return lax.dot_general(left, right, (((1,), (1,)), ((), ())), preferred_element_type=jnp.float32)


def start_all(pairs, sems):
    copies = [pltpu.make_async_copy(source, target, sems.at[turn]) for turn, (source, target) in enumerate(pairs)]
    for copy in copies:
        copy.start()
    return copies


def clear_counts(count, bands):
    def clear(owner, _):
        count[owner] = 0
        return 0

    lax.fori_loop(0, bands, clear, 0)


def overflow_mark(route, count):
    mark = jnp.int32(0)
    for block in range(NB):
        owner = route[block]
        seen = count[owner]
        count[owner] = seen + 1
        mark = jnp.where(seen == DIRECT, jnp.where(mark == 0, owner + 1, MANY), mark)
    return mark


def pack_kernel(
    bands, shared,
    route_hbm, slot_hbm, u_hbm, v_hbm, vis_hbm, uo_hbm, vo_hbm, out_ref,
    route, slot, u_ref, v_ref, vis_ref, uo_ref, vo_ref, count, sems,
):
    copies = start_all(
        (
            (route_hbm, route), (slot_hbm, slot), (u_hbm, u_ref), (v_hbm, v_ref),
            (vis_hbm, vis_ref), (uo_hbm, uo_ref), (vo_hbm, vo_ref),
        ),
        sems,
    )
    per_owner = DIRECT * TILES
    clear_counts(count, bands)
    copies[0].wait()
    copies[1].wait()
    mark = jnp.int32(0)
    if shared:
        mark = overflow_mark(route, count)
        clear_counts(count, bands)
    marks = jnp.broadcast_to(mark, (1, TS)).astype(jnp.float32)
    nothing = jnp.zeros((7, TS), jnp.float32)
    blank = jnp.concatenate([nothing, marks, nothing, marks], axis=0).astype(jnp.bfloat16)
    empty = jnp.zeros((16, TS), jnp.bfloat16)
    for target in range(bands * DIRECT):
        for tile in range(TILES - 1):
            out_ref[target * TILES + tile] = empty
        out_ref[target * TILES + TILES - 1] = blank
    for copy in copies[2:]:
        copy.wait()

    for block in range(NB):
        owner = route[block]
        rank = count[owner]
        count[owner] = rank + 1
        base = owner * per_owner + rank * TILES

        @pl.when((owner + 1 != mark) & (rank < DIRECT))
        def _():
            place = jnp.full((1, TS), slot[block] + 1, jnp.int32).astype(jnp.float32)
            misc = []
            for half in range(2):
                lanes = slice(block * BLOCK + half * TS, block * BLOCK + half * TS + TS)
                row = block * 2 + half
                out_ref[base + half] = u_ref[:, lanes]
                out_ref[base + 2 + half] = v_ref[:, lanes]
                misc += [
                    vis_ref[0, :, lanes].astype(jnp.float32),
                    vis_ref[1, :, lanes].astype(jnp.float32),
                    uo_ref[row:row + 1, :].astype(jnp.float32),
                    vo_ref[row:row + 1, :].astype(jnp.float32),
                    place,
                    marks,
                ]
            out_ref[base + 4] = jnp.concatenate(misc, axis=0).astype(jnp.bfloat16)


def own_kernel(
    bands,
    route_hbm, slot_hbm, u_hbm, v_hbm, vis_hbm, uo_hbm, vo_hbm, out_0, out_1, out_2, out_3,
    route, slot, u_ref, v_ref, vis_ref, uo_ref, vo_ref, count, listed, grid, sems,
):
    copies = start_all(
        (
            (route_hbm, route), (slot_hbm, slot), (u_hbm, u_ref), (v_hbm, v_ref), (vis_hbm, vis_ref),
            (uo_hbm, uo_ref), (vo_hbm, vo_ref),
        ),
        sems,
    )
    grid[...] = jnp.zeros_like(grid)
    clear_counts(count, bands)
    copies[0].wait()
    copies[1].wait()
    mark = overflow_mark(route, count)
    filled = jnp.int32(0)
    for block in range(NB):
        listed[filled] = block
        filled = filled + (route[block] + 1 == mark).astype(jnp.int32)
    for copy in copies[2:]:
        copy.wait()

    def add_block(turn, _):
        block = listed[turn]
        halves = []
        for half in range(2):
            lanes = pl.ds(pl.multiple_of(block * BLOCK + half * TS, TS), TS)
            row = pl.ds(block * 2 + half, 1)
            own = jnp.concatenate(
                [
                    vis_ref[0, :, lanes].astype(jnp.float32),
                    vis_ref[1, :, lanes].astype(jnp.float32),
                    uo_ref[row, :].astype(jnp.float32),
                    vo_ref[row, :].astype(jnp.float32),
                ],
                axis=0,
            )
            halves.append((u_ref[:, lanes].astype(jnp.float32), v_ref[:, lanes].astype(jnp.float32), own))
        cells = pl.ds(pl.multiple_of(slot[block] * TS, TS), TS)
        grid[:, cells] += block_tile(halves)
        return 0

    lax.fori_loop(0, filled, add_block, 0)
    me = lax.axis_index("tile") % PEERS
    width = TS // PEERS
    for turn, out_ref in enumerate((out_0, out_1, out_2, out_3)):
        first = pl.multiple_of((me ^ turn) * width, width)
        for part in range(2):
            out_ref[part * width:(part + 1) * width, :] = grid[pl.ds(part * TS + first, width), :].astype(jnp.bfloat16)


def own_columns_kernel(got_0, got_1, got_2, got_3, table_hbm, out_ref, table, sem):
    copy = pltpu.make_async_copy(table_hbm, table, sem)
    copy.start()
    total = got_0[...].astype(jnp.float32)
    for got_ref in (got_1, got_2, got_3):
        total += got_ref[...].astype(jnp.float32)
    both = turned_parts(total.astype(jnp.bfloat16))
    rows = IMY // out_ref.shape[0]
    step = 256
    copy.wait()
    for first in range(0, IMY, step):
        part = dot_rows(table[first:first + step, :], both)
        for row in range(0, step, rows):
            pieces = [part[row:row + rows // 2], part[row + rows // 2:row + rows]]
            out_ref[(first + row) // rows] = jnp.concatenate(pieces, axis=1).astype(jnp.bfloat16)


def got_tile(got_ref, base):
    misc = got_ref[base + 4].astype(jnp.float32)
    halves = [
        (got_ref[base + half].astype(jnp.float32), got_ref[base + 2 + half].astype(jnp.float32), misc[8 * half:8 * half + 8])
        for half in range(2)
    ]
    return misc, block_tile(halves)


def turned_parts(rounded):
    half = rounded.shape[0] // 2
    return jnp.concatenate([rounded, jnp.concatenate([-rounded[half:], rounded[:half]], axis=0)], axis=1)


def write_columns(grid, table, out_ref):
    both = turned_parts(grid[...].astype(jnp.bfloat16))
    rows = IMY // out_ref.shape[0]
    step = 256
    for first in range(0, IMY, step):
        part = dot_rows(table[first:first + step, :], both)
        for row in range(0, step, rows):
            pieces = [part[row:row + rows, :TS], part[row:row + rows, TS:]]
            out_ref[(first + row) // rows, :2 * rows, :] = jnp.concatenate(pieces, axis=0).astype(jnp.bfloat16)


def full_grid_kernel(places, got_ref, table_hbm, out_ref, grid, table, sem):
    copy = pltpu.make_async_copy(table_hbm, table, sem)
    copy.start()
    grid[...] = jnp.zeros_like(grid)
    tiles = got_ref.shape[0]

    def add_slot(index, _):
        @pl.when(places[index] > 0)
        def _():
            cells = pl.ds(pl.multiple_of((places[index] - 1) * TS, TS), TS)
            grid[:, cells] += got_tile(got_ref, index * TILES)[1]

        return 0

    lax.fori_loop(0, tiles // TILES, add_slot, 0)
    out_ref[...] = jnp.zeros_like(out_ref)
    copy.wait()
    write_columns(grid, table, out_ref)


def grid_kernel(bands, shared, got_ref, *refs):
    if shared:
        partial, table_hbm, out_ref, flags, grid, table, sem = refs
    else:
        table_hbm, out_ref, flags, grid, table, sem = refs
    copy = pltpu.make_async_copy(table_hbm, table, sem)
    copy.start()
    grid[...] = jnp.zeros_like(grid)
    per_owner = DIRECT * TILES

    def add_source(source, carried):
        least, most = carried
        for rank in range(DIRECT):
            misc, tile = got_tile(got_ref, source * per_owner + rank * TILES)
            place = jnp.maximum(misc[6, 0].astype(jnp.int32) - 1, 0)
            cells = pl.ds(pl.multiple_of(place * TS, TS), TS)
            grid[:, cells] += tile
        marks = misc[:8]
        return jnp.minimum(least, jnp.where(marks == 0.0, float(MANY), marks)), jnp.maximum(most, marks)

    start = (jnp.full((8, TS), float(MANY), jnp.float32), jnp.zeros((8, TS), jnp.float32))
    least, most = lax.fori_loop(0, bands, add_source, start, unroll=4)
    low, high = least[7, 0].astype(jnp.int32), most[7, 0].astype(jnp.int32)
    flags[0] = ((high == 0) | ((low == high) & (high != MANY))).astype(jnp.int32)
    flags[1] = jnp.where(high == MANY, 0, jnp.maximum(high - 1, 0))
    if shared:
        out_ref[:, out_ref.shape[1] - 16:, :] = partial[...]
    copy.wait()
    write_columns(grid, table, out_ref)


def side_by_side(got_ref, band, group, first, rows):
    return jnp.concatenate(
        [got_ref[band, group, first:first + rows, :], got_ref[band, group, first + rows:first + 2 * rows, :]], axis=1
    )


def band_dot(got_ref, table_ref, rows, copies=()):
    total = None
    for band in range(got_ref.shape[0]):
        both = jnp.concatenate([side_by_side(got_ref, band, group, 0, rows) for group in range(got_ref.shape[1])], axis=0)
        if copies:
            copies[band].wait()
        part = jnp.dot(
            both, table_ref[band * 2 * TS:(band + 1) * 2 * TS, :], preferred_element_type=jnp.float32
        )
        total = part if total is None else total + part
    return total


def image_kernel(scale, flags, got_ref, table_hbm, out_ref, table_ref, total, sems):
    rows = out_ref.shape[0]
    bands, groups = got_ref.shape[:2]
    pairs = []
    for band in range(bands):
        lines = pl.ds(band * 2 * TS, 2 * TS)
        pairs.append((table_hbm.at[lines, :], table_ref.at[lines, :]))
    total[...] = band_dot(got_ref, table_ref, rows, start_all(pairs, sems))
    width = TS // PEERS
    left, right = [], []
    for peer in range(PEERS):
        per_group = []
        for group in range(groups):
            added = got_ref[peer, group, 2 * rows:, :].astype(jnp.float32)
            for band in range(peer + PEERS, bands, PEERS):
                added += got_ref[band, group, 2 * rows:, :].astype(jnp.float32)
            per_group += [added[:, :2 * width], added[:, 2 * width:]]
        left.append(jnp.concatenate(per_group, axis=0))
        for part in range(2):
            first = pl.multiple_of((flags[1] * 2 + part) * TS + peer * width, width)
            right.append(table_ref[pl.ds(first, width), :])
    total[...] += jnp.dot(
        jnp.concatenate(left, axis=1).astype(jnp.bfloat16),
        jnp.concatenate(right, axis=0),
        preferred_element_type=jnp.float32,
    )
    image = total[:rows]
    for group in range(1, groups):
        image = image + total[group * rows:(group + 1) * rows]
    out_ref[...] = image * scale


def plain_image_kernel(scale, got_ref, table_ref, out_ref, total):
    turn = pl.program_id(0)

    @pl.when(turn == 0)
    def _():
        total[...] = jnp.zeros_like(total)

    rows = out_ref.shape[0]
    total[...] += band_dot(got_ref, table_ref, rows)

    @pl.when(turn == pl.num_programs(0) - 1)
    def _():
        out_ref[...] = (total[:rows] + total[rows:]) * scale


VMEM = pl.BlockSpec(memory_space=pltpu.VMEM)
SMEM = pl.BlockSpec(memory_space=pltpu.SMEM)
HBM = pl.BlockSpec(memory_space=pltpu.HBM)
PARAMS = pltpu.CompilerParams(vmem_limit_bytes=20 * 1024 * 1024)


def body(visibility, u_kernel, v_kernel, u_offset, v_offset, tile_route, tile_slot):
    bands = lax.axis_size("tile")
    groups = lax.axis_size("chan")
    local_rows = visibility.shape[2]
    capacity = 4 * NB // bands
    shared = capacity > DIRECT
    rows_y = IMY // (bands * groups)
    sent_rows = 2 * rows_y + (16 if shared else 0)
    columns_shape = jax.ShapeDtypeStruct((bands * groups, sent_rows, TS), jnp.bfloat16)
    v_table = jnp.asarray(column_table())
    operands = (
        tile_route[:, 0],
        tile_slot,
        u_kernel.reshape(2 * KS, local_rows),
        v_kernel.reshape(2 * KS, local_rows),
        visibility,
        u_offset.reshape(NB * 2, TS),
        v_offset.reshape(NB * 2, TS),
    )
    grid_scratch = [
        pltpu.VMEM((2 * TS, TPD * TS), jnp.float32),
        pltpu.VMEM((IMY, 2 * TPD * TS), jnp.bfloat16),
        pltpu.SemaphoreType.DMA,
    ]
    raw_scratch = [
        pltpu.SMEM((NB,), jnp.int32),
        pltpu.SMEM((NB,), jnp.int32),
        pltpu.VMEM((2 * KS, local_rows), jnp.bfloat16),
        pltpu.VMEM((2 * KS, local_rows), jnp.bfloat16),
        pltpu.VMEM(visibility.shape, jnp.bfloat16),
        pltpu.VMEM((NB * 2, TS), jnp.int32),
        pltpu.VMEM((NB * 2, TS), jnp.int32),
    ]
    packed = pl.pallas_call(
        functools.partial(pack_kernel, bands, shared),
        out_shape=jax.ShapeDtypeStruct((bands * DIRECT * TILES, 16, TS), jnp.bfloat16),
        in_specs=[HBM] * 7,
        out_specs=VMEM,
        scratch_shapes=raw_scratch + [pltpu.SMEM((bands,), jnp.int32), pltpu.SemaphoreType.DMA((7,))],
        compiler_params=PARAMS,
    )(*operands)
    got = lax.all_to_all(packed, "tile", split_axis=0, concat_axis=0, tiled=True)
    partial = ()
    if shared:
        own = pl.pallas_call(
            functools.partial(own_kernel, bands),
            out_shape=[jax.ShapeDtypeStruct((2 * TS // PEERS, TPD * TS), jnp.bfloat16)] * PEERS,
            in_specs=[HBM] * 7,
            out_specs=[VMEM] * PEERS,
            scratch_shapes=raw_scratch + [
                pltpu.SMEM((bands,), jnp.int32),
                pltpu.SMEM((NB + 1,), jnp.int32),
                pltpu.VMEM((2 * TS, TPD * TS), jnp.float32),
                pltpu.SemaphoreType.DMA((7,)),
            ],
            compiler_params=PARAMS,
            cost_estimate=pl.CostEstimate(flops=10 ** 9, bytes_accessed=2 * 10 ** 6, transcendentals=0),
        )(*operands)
        summed = [own[0]] + [
            lax.ppermute(own[turn], "tile", [(band, band ^ turn) for band in range(bands)]) for turn in range(1, PEERS)
        ]
        partial = (
            pl.pallas_call(
                own_columns_kernel,
                out_shape=jax.ShapeDtypeStruct((bands * groups, 16, TS), jnp.bfloat16),
                in_specs=[VMEM] * PEERS + [HBM],
                out_specs=VMEM,
                scratch_shapes=[pltpu.VMEM((IMY, 2 * TPD * TS), jnp.bfloat16), pltpu.SemaphoreType.DMA],
                compiler_params=PARAMS,
                cost_estimate=pl.CostEstimate(flops=10 ** 9, bytes_accessed=5 * 10 ** 6, transcendentals=0),
            )(*summed, v_table),
        )
    columns, flags = pl.pallas_call(
        functools.partial(grid_kernel, bands, shared),
        out_shape=(columns_shape, jax.ShapeDtypeStruct((2,), jnp.int32)),
        in_specs=[VMEM] * (1 + len(partial)) + [HBM],
        out_specs=(VMEM, SMEM),
        scratch_shapes=grid_scratch,
        compiler_params=PARAMS,
    )(got, *partial, v_table)

    def every_slot(_):
        slots = bands * capacity
        packed = pl.pallas_call(
            functools.partial(full_pack_kernel, capacity),
            out_shape=jax.ShapeDtypeStruct((slots * TILES, 16, TS), jnp.bfloat16),
            in_specs=[SMEM, SMEM, VMEM, VMEM, VMEM, VMEM, VMEM],
            out_specs=VMEM,
            scratch_shapes=[pltpu.SMEM((bands,), jnp.int32)],
            compiler_params=PARAMS,
        )(*operands)
        got = lax.all_to_all(packed, "tile", split_axis=0, concat_axis=0, tiled=True)
        places = got.reshape(slots, TILES, 16, TS)[:, TILES - 1, 6, 0].astype(jnp.int32)
        return pl.pallas_call(
            full_grid_kernel,
            out_shape=columns_shape,
            in_specs=[SMEM, VMEM, HBM],
            out_specs=VMEM,
            scratch_shapes=grid_scratch,
            compiler_params=PARAMS,
        )(places, got, v_table)

    if shared:
        columns = lax.cond(flags[0] == 1, lambda kept: kept, every_slot, columns)
    sent = lax.all_to_all(columns, ("tile", "chan"), split_axis=0, concat_axis=0, tiled=True)
    sent = sent.reshape(bands, groups, sent_rows, TS)
    scale = 1.0 / (KS * KS * math.sqrt(local_rows * bands * CH))
    out_shape = jax.ShapeDtypeStruct((rows_y, IMX), jnp.float32)
    if shared:
        u_table = jnp.asarray(np.pad(image_table(bands), ((0, 2048), (0, 0))))
        return pl.pallas_call(
            functools.partial(image_kernel, scale),
            out_shape=out_shape,
            in_specs=[SMEM, VMEM, HBM],
            out_specs=VMEM,
            scratch_shapes=[
                pltpu.VMEM((bands * 2 * TS, IMX), jnp.bfloat16),
                pltpu.VMEM((groups * rows_y, IMX), jnp.float32),
                pltpu.SemaphoreType.DMA((bands,)),
            ],
            compiler_params=pltpu.CompilerParams(vmem_limit_bytes=52 * 1024 * 1024),
        )(flags, sent, u_table)
    per_turn = 4
    return pl.pallas_call(
        functools.partial(plain_image_kernel, scale),
        out_shape=out_shape,
        grid=(bands // per_turn,),
        in_specs=[
            pl.BlockSpec((per_turn, groups, sent_rows, TS), lambda turn: (turn, 0, 0, 0)),
            pl.BlockSpec((per_turn * 2 * TS, IMX), lambda turn: (turn, 0)),
        ],
        out_specs=pl.BlockSpec((rows_y, IMX), lambda turn: (0, 0)),
        scratch_shapes=[pltpu.VMEM((groups * rows_y, IMX), jnp.float32)],
        compiler_params=PARAMS,
    )(sent, jnp.asarray(image_table(bands)))


def solution(mesh):
    placed = (
        P("chan", None, "tile"),
        P("chan", None, "tile"),
        P("chan", None, "tile"),
        P("tile"),
        P("tile"),
        P("tile", None),
        P("tile"),
    )
    return jax.shard_map(
        body, mesh=mesh, in_specs=placed, out_specs=P(("tile", "chan"), None), check_vma=False
    )
```

```python
import functools
import math

import jax
import jax.numpy as jnp
import ml_dtypes
import numpy as np
from jax import lax
from jax.experimental import pallas as pl
from jax.experimental.pallas import tpu as pltpu
from jax.sharding import PartitionSpec as P

NG = 16384
CH = 4
KS = 8
BLOCK = 256
TS = 128
TPD = 8
NB = 32
IMX = 1024
IMY = 1024
ROWS = 80
TILES = ROWS // 16
DIRECT = 2
HELD = 4
PEERS = 4
MANY = 255


def phase_table(rows_coord, cols_coord):
    turns = np.mod(rows_coord[:, None].astype(np.int64) * cols_coord[None, :].astype(np.int64), NG)
    angles = turns.astype(np.float64) * (2.0 * math.pi / NG)
    return np.cos(angles).astype(ml_dtypes.bfloat16), np.sin(angles).astype(ml_dtypes.bfloat16)


def column_table():
    cos_v, sin_v = phase_table(np.arange(IMY) - IMY // 2, np.arange(TPD * TS))
    return np.concatenate([cos_v, sin_v], axis=1)


def image_table(bands):
    cos_u, sin_u = phase_table(np.arange(bands * TS), np.arange(IMX) - IMX // 2)
    both = np.stack([cos_u.reshape(bands, TS, IMX), (-sin_u).reshape(bands, TS, IMX)], axis=1)
    return both.reshape(bands * 2 * TS, IMX)


def full_pack_kernel(capacity, route, slot, u_ref, v_ref, vis_ref, uo_ref, vo_ref, out_ref, count):
    owners = out_ref.shape[0] // (capacity * TILES)
    out_ref[...] = jnp.zeros_like(out_ref)

    def clear(owner, _):
        count[owner] = 0
        return 0

    lax.fori_loop(0, owners, clear, 0)
    for block in range(NB):
        owner = route[block]
        rank = count[owner]
        count[owner] = rank + 1
        base = (owner * capacity + rank) * TILES
        place = jnp.full((1, TS), slot[block] + 1, jnp.int32).astype(jnp.float32)
        misc = []
        for half in range(2):
            lanes = slice(block * BLOCK + half * TS, block * BLOCK + half * TS + TS)
            row = block * 2 + half
            out_ref[base + half] = u_ref[:, lanes]
            out_ref[base + 2 + half] = v_ref[:, lanes]
            misc += [
                vis_ref[0, :, lanes].astype(jnp.float32),
                vis_ref[1, :, lanes].astype(jnp.float32),
                uo_ref[row:row + 1, :].astype(jnp.float32),
                vo_ref[row:row + 1, :].astype(jnp.float32),
                place,
                jnp.zeros((1, TS), jnp.float32),
            ]
        out_ref[base + 4] = jnp.concatenate(misc, axis=0).astype(jnp.bfloat16)


def turned(kernel, first):
    for bit in (1, 2, 4):
        kernel = jnp.where((first & bit) != 0, pltpu.roll(kernel, bit, 0), kernel)
    return kernel


def spread(kernel, first_tile):
    both = jnp.concatenate([kernel, kernel], axis=0).astype(jnp.bfloat16)
    zero = jnp.zeros_like(both)
    return jnp.concatenate(
        [jnp.where(first_tile == pair * 2, both, zero) for pair in range(TS // 16)], axis=0
    )


def tile_of(first):
    sub = lax.broadcasted_iota(jnp.int32, (8, TS), 0)
    tile = lax.shift_right_logical(first + ((sub - first) & 7), 3)
    return jnp.concatenate([tile, tile - 1], axis=0).astype(jnp.float32).astype(jnp.bfloat16)


def block_tile(halves):
    v_parts, w_parts = [], []
    for u_two, v_two, own in halves:
        u_first = jnp.broadcast_to(own[4:5], (8, TS)).astype(jnp.int32)
        v_first = jnp.broadcast_to(own[5:6], (8, TS)).astype(jnp.int32)
        u_tile, v_tile = tile_of(u_first), tile_of(v_first)
        for chan in range(2):
            v_parts.append(spread(turned(v_two[8 * chan:8 * chan + 8], v_first), v_tile))
            u_turned = turned(u_two[8 * chan:8 * chan + 8], u_first)
            w_parts.append(jnp.concatenate(
                [spread(u_turned * own[2 * chan + part:2 * chan + part + 1], u_tile) for part in range(2)],
                axis=0,
            ))
    return dot_rows(jnp.concatenate(w_parts, axis=1), jnp.concatenate(v_parts, axis=1))


def dot_rows(left, right):
    return lax.dot_general(left, right, (((1,), (1,)), ((), ())), preferred_element_type=jnp.float32)


def start_all(pairs, sems):
    copies = [pltpu.make_async_copy(source, target, sems.at[turn]) for turn, (source, target) in enumerate(pairs)]
    for copy in copies:
        copy.start()
    return copies


def clear_counts(count, bands):
    def clear(owner, _):
        count[owner] = 0
        return 0

    lax.fori_loop(0, bands, clear, 0)


def overflow_mark(route, count):
    mark = jnp.int32(0)
    for block in range(NB):
        owner = route[block]
        seen = count[owner]
        count[owner] = seen + 1
        mark = jnp.where(seen == DIRECT, jnp.where(mark == 0, owner + 1, MANY), mark)
    return mark


def pack_kernel(
    bands, shared,
    route_hbm, slot_hbm, u_hbm, v_hbm, vis_hbm, uo_hbm, vo_hbm, out_ref,
    route, slot, u_ref, v_ref, vis_ref, uo_ref, vo_ref, count, sems,
):
    copies = start_all(
        (
            (route_hbm, route), (slot_hbm, slot), (u_hbm, u_ref), (v_hbm, v_ref),
            (vis_hbm, vis_ref), (uo_hbm, uo_ref), (vo_hbm, vo_ref),
        ),
        sems,
    )
    per_owner = DIRECT * TILES
    clear_counts(count, bands)
    copies[0].wait()
    copies[1].wait()
    mark = jnp.int32(0)
    if shared:
        mark = overflow_mark(route, count)
        clear_counts(count, bands)
    marks = jnp.broadcast_to(mark, (1, TS)).astype(jnp.float32)
    nothing = jnp.zeros((7, TS), jnp.float32)
    blank = jnp.concatenate([nothing, marks, nothing, marks], axis=0).astype(jnp.bfloat16)
    empty = jnp.zeros((16, TS), jnp.bfloat16)
    for target in range(bands * DIRECT):
        for tile in range(TILES - 1):
            out_ref[target * TILES + tile] = empty
        out_ref[target * TILES + TILES - 1] = blank
    for copy in copies[2:]:
        copy.wait()

    for block in range(NB):
        owner = route[block]
        rank = count[owner]
        count[owner] = rank + 1
        base = owner * per_owner + rank * TILES

        @pl.when((owner + 1 != mark) & (rank < DIRECT))
        def _():
            place = jnp.full((1, TS), slot[block] + 1, jnp.int32).astype(jnp.float32)
            misc = []
            for half in range(2):
                lanes = slice(block * BLOCK + half * TS, block * BLOCK + half * TS + TS)
                row = block * 2 + half
                out_ref[base + half] = u_ref[:, lanes]
                out_ref[base + 2 + half] = v_ref[:, lanes]
                misc += [
                    vis_ref[0, :, lanes].astype(jnp.float32),
                    vis_ref[1, :, lanes].astype(jnp.float32),
                    uo_ref[row:row + 1, :].astype(jnp.float32),
                    vo_ref[row:row + 1, :].astype(jnp.float32),
                    place,
                    marks,
                ]
            out_ref[base + 4] = jnp.concatenate(misc, axis=0).astype(jnp.bfloat16)


def own_kernel(
    bands,
    route_hbm, slot_hbm, u_hbm, v_hbm, vis_hbm, uo_hbm, vo_hbm, share_0, share_1, share_2, share_3,
    route, slot, u_ref, v_ref, vis_ref, uo_ref, vo_ref, count, sems, listed, grid,
):
    copies = start_all(
        (
            (route_hbm, route), (slot_hbm, slot), (u_hbm, u_ref), (v_hbm, v_ref),
            (vis_hbm, vis_ref), (uo_hbm, uo_ref), (vo_hbm, vo_ref),
        ),
        sems,
    )
    grid[...] = jnp.zeros_like(grid)
    clear_counts(count, bands)
    copies[0].wait()
    copies[1].wait()
    mark = overflow_mark(route, count)
    filled = jnp.int32(0)
    for block in range(NB):
        listed[filled] = block
        filled = filled + (route[block] + 1 == mark).astype(jnp.int32)
    for copy in copies[2:]:
        copy.wait()

    def own_tile(block, used):
        halves = []
        for half in range(2):
            lanes = pl.ds(pl.multiple_of(block * BLOCK + half * TS, TS), TS)
            row = pl.ds(block * 2 + half, 1)
            own = jnp.concatenate(
                [
                    vis_ref[0, :, lanes].astype(jnp.float32) * used,
                    vis_ref[1, :, lanes].astype(jnp.float32) * used,
                    uo_ref[row, :].astype(jnp.float32),
                    vo_ref[row, :].astype(jnp.float32),
                ],
                axis=0,
            )
            halves.append((u_ref[:, lanes].astype(jnp.float32), v_ref[:, lanes].astype(jnp.float32), own))
        return block_tile(halves)

    def add_blocks(turn, _):
        for lane in range(4):
            number = turn * 4 + lane
            block = listed[jnp.minimum(number, filled - 1)]
            cells = pl.ds(pl.multiple_of(slot[block] * TS, TS), TS)
            grid[:, cells] += own_tile(block, (number < filled).astype(jnp.float32))
        return 0

    lax.fori_loop(0, (filled + 3) // 4, add_blocks, 0)
    me = lax.axis_index("tile") % PEERS
    width = TS // PEERS
    for turn, share_ref in enumerate((share_0, share_1, share_2, share_3)):
        first = pl.multiple_of((me ^ turn) * width, width)
        for part in range(2):
            share_ref[part * width:(part + 1) * width, :] = grid[pl.ds(part * TS + first, width), :].astype(jnp.bfloat16)


def hold_kernel(flags, table_hbm, *refs):
    parts, own, sems = refs[:-2], refs[-2], refs[-1]
    rows = parts[0].shape[0]
    pairs = [(table_hbm.at[pl.ds(turn * rows, rows), :], part) for turn, part in enumerate(parts)]
    width = TS // PEERS
    for turn in range(2 * PEERS):
        peer, part = turn // 2, turn % 2
        first = pl.multiple_of((flags[1] * 2 + part) * TS + peer * width, width)
        pairs.append((table_hbm.at[pl.ds(first, width), :], own.at[pl.ds(turn * width, width), :]))
    for copy in start_all(pairs, sems):
        copy.wait()


def got_tile(got_ref, base):
    misc = got_ref[base + 4].astype(jnp.float32)
    halves = [
        (got_ref[base + half].astype(jnp.float32), got_ref[base + 2 + half].astype(jnp.float32), misc[8 * half:8 * half + 8])
        for half in range(2)
    ]
    return misc, block_tile(halves)


def turned_parts(rounded):
    half = rounded.shape[0] // 2
    return jnp.concatenate([rounded, jnp.concatenate([-rounded[half:], rounded[:half]], axis=0)], axis=1)


def write_columns(grid, table, out_ref, own=None):
    both = turned_parts(grid[...].astype(jnp.bfloat16))
    if own is not None:
        both = jnp.concatenate([both, turned_parts(own)], axis=0)
    rows = IMY // out_ref.shape[0]
    step = 256
    for first in range(0, IMY, step):
        part = dot_rows(table[first:first + step, :], both)
        for row in range(0, step, rows):
            pieces = [part[row:row + rows, :TS], part[row:row + rows, TS:2 * TS]]
            if own is not None:
                middle = row + rows // 2
                pieces.append(jnp.concatenate([part[row:middle, 2 * TS:], part[middle:row + rows, 2 * TS:]], axis=1))
            out_ref[(first + row) // rows, :rows * 2 + (16 if own is not None else 0), :] = jnp.concatenate(
                pieces, axis=0
            ).astype(jnp.bfloat16)


def full_grid_kernel(places, got_ref, table_hbm, out_ref, grid, table, sem):
    copy = pltpu.make_async_copy(table_hbm, table, sem)
    copy.start()
    grid[...] = jnp.zeros_like(grid)
    tiles = got_ref.shape[0]

    def add_slot(index, _):
        @pl.when(places[index] > 0)
        def _():
            cells = pl.ds(pl.multiple_of((places[index] - 1) * TS, TS), TS)
            grid[:, cells] += got_tile(got_ref, index * TILES)[1]

        return 0

    lax.fori_loop(0, tiles // TILES, add_slot, 0)
    out_ref[...] = jnp.zeros_like(out_ref)
    copy.wait()
    write_columns(grid, table, out_ref)


def grid_kernel(bands, shared, got_ref, *refs):
    shares = refs[:PEERS] if shared else ()
    table_hbm, out_ref, flags, grid, table, sem = refs[len(shares):]
    copy = pltpu.make_async_copy(table_hbm, table, sem)
    copy.start()
    grid[...] = jnp.zeros_like(grid)
    per_owner = DIRECT * TILES

    def add_source(source, carried):
        least, most = carried
        for rank in range(DIRECT):
            misc, tile = got_tile(got_ref, source * per_owner + rank * TILES)
            place = jnp.maximum(misc[6, 0].astype(jnp.int32) - 1, 0)
            cells = pl.ds(pl.multiple_of(place * TS, TS), TS)
            grid[:, cells] += tile
        marks = misc[:8]
        return jnp.minimum(least, jnp.where(marks == 0.0, float(MANY), marks)), jnp.maximum(most, marks)

    start = (jnp.full((8, TS), float(MANY), jnp.float32), jnp.zeros((8, TS), jnp.float32))
    least, most = lax.fori_loop(0, bands, add_source, start, unroll=4)
    low, high = least[7, 0].astype(jnp.int32), most[7, 0].astype(jnp.int32)
    flags[0] = ((high == 0) | ((low == high) & (high != MANY))).astype(jnp.int32)
    flags[1] = jnp.where(high == MANY, 0, jnp.maximum(high - 1, 0))
    own = None
    if shared:
        own = shares[0][...].astype(jnp.float32)
        for share in shares[1:]:
            own += share[...].astype(jnp.float32)
        own = own.astype(jnp.bfloat16)
    copy.wait()
    write_columns(grid, table, out_ref, own)


def side_by_side(got_ref, band, group, first, rows):
    return jnp.concatenate(
        [got_ref[band, group, first:first + rows, :], got_ref[band, group, first + rows:first + 2 * rows, :]], axis=1
    )


def band_dot(got_ref, table, rows, bands):
    left = jnp.concatenate(
        [
            jnp.concatenate([side_by_side(got_ref, band, group, 0, rows) for band in bands], axis=1)
            for group in range(got_ref.shape[1])
        ],
        axis=0,
    )
    return jnp.dot(left, table, preferred_element_type=jnp.float32)


def image_kernel(scale, got_ref, *refs):
    held = refs[:HELD]
    own_ref, table_hbm, out_ref, table_ref, sems = refs[HELD:]
    rows = out_ref.shape[0]
    bands, groups = got_ref.shape[:2]
    pairs = []
    for band in range(HELD, bands):
        lines = pl.ds(band * 2 * TS, 2 * TS)
        pairs.append((table_hbm.at[lines, :], table_ref.at[pl.ds((band - HELD) * 2 * TS, 2 * TS), :]))
    copies = start_all(pairs, sems)
    width = TS // PEERS
    left = []
    for peer in range(PEERS):
        per_group = []
        for group in range(groups):
            added = got_ref[peer, group, 2 * rows:, :].astype(jnp.float32)
            for band in range(peer + PEERS, bands, PEERS):
                added += got_ref[band, group, 2 * rows:, :].astype(jnp.float32)
            per_group += [added[:, :2 * width], added[:, 2 * width:]]
        left.append(jnp.concatenate(per_group, axis=0))
    total = jnp.dot(
        jnp.concatenate(left, axis=1).astype(jnp.bfloat16), own_ref[...], preferred_element_type=jnp.float32
    )
    table = jnp.concatenate([part[...] for part in held], axis=0)
    total = total + band_dot(got_ref, table, rows, range(HELD))
    for first in range(HELD, bands, HELD):
        for band in range(first, first + HELD):
            copies[band - HELD].wait()
        table = table_ref[(first - HELD) * 2 * TS:first * 2 * TS, :]
        total = total + band_dot(got_ref, table, rows, range(first, first + HELD))
    image = total[:rows]
    for group in range(1, groups):
        image = image + total[group * rows:(group + 1) * rows]
    out_ref[...] = image * scale


def plain_image_kernel(scale, got_ref, table_ref, out_ref, total):
    turn = pl.program_id(0)

    @pl.when(turn == 0)
    def _():
        total[...] = jnp.zeros_like(total)

    rows = out_ref.shape[0]
    part = total[...] + band_dot(got_ref, table_ref[...], rows, range(got_ref.shape[0]))
    total[...] = part

    @pl.when(turn == pl.num_programs(0) - 1)
    def _():
        out_ref[...] = (part[:rows] + part[rows:]) * scale


VMEM = pl.BlockSpec(memory_space=pltpu.VMEM)
SMEM = pl.BlockSpec(memory_space=pltpu.SMEM)
HBM = pl.BlockSpec(memory_space=pltpu.HBM)
PARAMS = pltpu.CompilerParams(vmem_limit_bytes=20 * 1024 * 1024)


def body(visibility, u_kernel, v_kernel, u_offset, v_offset, tile_route, tile_slot):
    bands = lax.axis_size("tile")
    groups = lax.axis_size("chan")
    local_rows = visibility.shape[2]
    capacity = 4 * NB // bands
    shared = capacity > DIRECT
    rows_y = IMY // (bands * groups)
    sent_rows = 2 * rows_y + (16 if shared else 0)
    columns_shape = jax.ShapeDtypeStruct((bands * groups, sent_rows, TS), jnp.bfloat16)
    v_table = jnp.asarray(column_table())
    operands = (
        tile_route[:, 0],
        tile_slot,
        u_kernel.reshape(2 * KS, local_rows),
        v_kernel.reshape(2 * KS, local_rows),
        visibility,
        u_offset.reshape(NB * 2, TS),
        v_offset.reshape(NB * 2, TS),
    )
    grid_scratch = [
        pltpu.VMEM((2 * TS, TPD * TS), jnp.float32),
        pltpu.VMEM((IMY, 2 * TPD * TS), jnp.bfloat16),
        pltpu.SemaphoreType.DMA,
    ]
    raw_scratch = [
        pltpu.SMEM((NB,), jnp.int32),
        pltpu.SMEM((NB,), jnp.int32),
        pltpu.VMEM((2 * KS, local_rows), jnp.bfloat16),
        pltpu.VMEM((2 * KS, local_rows), jnp.bfloat16),
        pltpu.VMEM(visibility.shape, jnp.bfloat16),
        pltpu.VMEM((NB * 2, TS), jnp.int32),
        pltpu.VMEM((NB * 2, TS), jnp.int32),
    ]
    raw_scratch += [pltpu.SMEM((bands,), jnp.int32), pltpu.SemaphoreType.DMA((7,))]
    packed = pl.pallas_call(
        functools.partial(pack_kernel, bands, shared),
        out_shape=jax.ShapeDtypeStruct((bands * DIRECT * TILES, 16, TS), jnp.bfloat16),
        in_specs=[HBM] * 7,
        out_specs=VMEM,
        scratch_shapes=raw_scratch,
        compiler_params=PARAMS,
    )(*operands)
    got = lax.all_to_all(packed, "tile", split_axis=0, concat_axis=0, tiled=True)
    u_table = jnp.asarray(image_table(bands))
    partial = ()
    if shared:
        own = pl.pallas_call(
            functools.partial(own_kernel, bands),
            out_shape=[jax.ShapeDtypeStruct((2 * TS // PEERS, TPD * TS), jnp.bfloat16)] * PEERS,
            in_specs=[HBM] * 7,
            out_specs=[VMEM] * PEERS,
            scratch_shapes=raw_scratch + [
                pltpu.SMEM((NB + 1,), jnp.int32), pltpu.VMEM((2 * TS, TPD * TS), jnp.float32)
            ],
            compiler_params=PARAMS,
            cost_estimate=pl.CostEstimate(flops=10 ** 9, bytes_accessed=2 * 10 ** 6, transcendentals=0),
        )(*operands)
        summed = [own[0]] + [
            lax.ppermute(own[turn], "tile", [(band, band ^ turn) for band in range(bands)]) for turn in range(1, PEERS)
        ]
        partial = tuple(summed)
    columns, flags = pl.pallas_call(
        functools.partial(grid_kernel, bands, shared),
        out_shape=(columns_shape, jax.ShapeDtypeStruct((2,), jnp.int32)),
        in_specs=[VMEM] * (1 + len(partial)) + [HBM],
        out_specs=(VMEM, SMEM),
        scratch_shapes=grid_scratch,
        compiler_params=PARAMS,
    )(got, *partial, v_table)

    scale = 1.0 / (KS * KS * math.sqrt(local_rows * bands * CH))
    image_shape = jax.ShapeDtypeStruct((rows_y, IMX), jnp.float32)

    def exchanged(columns):
        sent = lax.all_to_all(columns, ("tile", "chan"), split_axis=0, concat_axis=0, tiled=True)
        return sent.reshape(bands, groups, sent_rows, TS)

    def plain_image(columns):
        per_turn = 4
        return pl.pallas_call(
            functools.partial(plain_image_kernel, scale),
            out_shape=image_shape,
            grid=(bands // per_turn,),
            in_specs=[
                pl.BlockSpec((per_turn, groups, sent_rows, TS), lambda turn: (turn, 0, 0, 0)),
                pl.BlockSpec((per_turn * 2 * TS, IMX), lambda turn: (turn, 0)),
            ],
            out_specs=pl.BlockSpec((rows_y, IMX), lambda turn: (0, 0)),
            scratch_shapes=[pltpu.VMEM((groups * rows_y, IMX), jnp.float32)],
            compiler_params=PARAMS,
        )(exchanged(columns), u_table)

    if not shared:
        return plain_image(columns)

    def every_slot(_):
        slots = bands * capacity
        packed = pl.pallas_call(
            functools.partial(full_pack_kernel, capacity),
            out_shape=jax.ShapeDtypeStruct((slots * TILES, 16, TS), jnp.bfloat16),
            in_specs=[SMEM, SMEM, VMEM, VMEM, VMEM, VMEM, VMEM],
            out_specs=VMEM,
            scratch_shapes=[pltpu.SMEM((bands,), jnp.int32)],
            compiler_params=PARAMS,
        )(*operands)
        got = lax.all_to_all(packed, "tile", split_axis=0, concat_axis=0, tiled=True)
        places = got.reshape(slots, TILES, 16, TS)[:, TILES - 1, 6, 0].astype(jnp.int32)
        columns = pl.pallas_call(
            full_grid_kernel,
            out_shape=columns_shape,
            in_specs=[SMEM, VMEM, HBM],
            out_specs=VMEM,
            scratch_shapes=grid_scratch,
            compiler_params=PARAMS,
        )(places, got, v_table)
        return plain_image(columns)

    held = pl.pallas_call(
        hold_kernel,
        out_shape=[jax.ShapeDtypeStruct((2 * TS, IMX), jnp.bfloat16)] * HELD
        + [jax.ShapeDtypeStruct((2 * TS, IMX), jnp.bfloat16)],
        in_specs=[SMEM, HBM],
        out_specs=[VMEM] * (HELD + 1),
        scratch_shapes=[pltpu.SemaphoreType.DMA((HELD + 2 * PEERS,))],
        compiler_params=PARAMS,
        cost_estimate=pl.CostEstimate(flops=0, bytes_accessed=16 * 10 ** 6, transcendentals=0),
    )(flags, u_table)
    image = pl.pallas_call(
        functools.partial(image_kernel, scale),
        out_shape=image_shape,
        in_specs=[VMEM] * (HELD + 2) + [HBM],
        out_specs=VMEM,
        scratch_shapes=[
            pltpu.VMEM(((bands - HELD) * 2 * TS, IMX), jnp.bfloat16),
            pltpu.SemaphoreType.DMA((bands - HELD,)),
        ],
        compiler_params=PARAMS,
    )(exchanged(columns), *held, u_table)
    return lax.cond(flags[0] == 1, lambda kept: kept, every_slot, image)


def solution(mesh):
    placed = (
        P("chan", None, "tile"),
        P("chan", None, "tile"),
        P("chan", None, "tile"),
        P("tile"),
        P("tile"),
        P("tile", None),
        P("tile"),
    )
    return jax.shard_map(
        body, mesh=mesh, in_specs=placed, out_specs=P(("tile", "chan"), None), check_vma=False
    )
```

```python
import functools
import math

import jax
import jax.numpy as jnp
import ml_dtypes
import numpy as np
from jax import lax
from jax.experimental import pallas as pl
from jax.experimental.pallas import tpu as pltpu
from jax.sharding import PartitionSpec as P

NG = 16384
CH = 4
KS = 8
BLOCK = 256
TS = 128
TPD = 8
NB = 32
IMX = 1024
IMY = 1024
ROWS = 80
TILES = ROWS // 16
DIRECT = 2
HELD = 4
PEERS = 4
MANY = 255


def phase_table(rows_coord, cols_coord):
    turns = np.mod(rows_coord[:, None].astype(np.int64) * cols_coord[None, :].astype(np.int64), NG)
    angles = turns.astype(np.float64) * (2.0 * math.pi / NG)
    return np.cos(angles).astype(ml_dtypes.bfloat16), np.sin(angles).astype(ml_dtypes.bfloat16)


def column_table():
    cos_v, sin_v = phase_table(np.arange(IMY) - IMY // 2, np.arange(TPD * TS))
    return np.concatenate([cos_v, sin_v], axis=1)


def image_table(bands):
    cos_u, sin_u = phase_table(np.arange(bands * TS), np.arange(IMX) - IMX // 2)
    both = np.stack([cos_u.reshape(bands, TS, IMX), (-sin_u).reshape(bands, TS, IMX)], axis=1)
    return both.reshape(bands * 2 * TS, IMX)


def full_pack_kernel(capacity, route, slot, u_ref, v_ref, vis_ref, uo_ref, vo_ref, out_ref, count):
    owners = out_ref.shape[0] // (capacity * TILES)
    out_ref[...] = jnp.zeros_like(out_ref)

    def clear(owner, _):
        count[owner] = 0
        return 0

    lax.fori_loop(0, owners, clear, 0)
    for block in range(NB):
        owner = route[block]
        rank = count[owner]
        count[owner] = rank + 1
        base = (owner * capacity + rank) * TILES
        place = jnp.full((1, TS), slot[block] + 1, jnp.int32).astype(jnp.float32)
        misc = []
        for half in range(2):
            lanes = slice(block * BLOCK + half * TS, block * BLOCK + half * TS + TS)
            row = block * 2 + half
            out_ref[base + half] = u_ref[:, lanes]
            out_ref[base + 2 + half] = v_ref[:, lanes]
            misc += [
                vis_ref[0, :, lanes].astype(jnp.float32),
                vis_ref[1, :, lanes].astype(jnp.float32),
                uo_ref[row:row + 1, :].astype(jnp.float32),
                vo_ref[row:row + 1, :].astype(jnp.float32),
                place,
                jnp.zeros((1, TS), jnp.float32),
            ]
        out_ref[base + 4] = jnp.concatenate(misc, axis=0).astype(jnp.bfloat16)


def turned(kernel, first):
    for bit in (1, 2, 4):
        kernel = jnp.where((first & bit) != 0, pltpu.roll(kernel, bit, 0), kernel)
    return kernel


def spread(kernel, first_tile):
    both = jnp.concatenate([kernel, kernel], axis=0).astype(jnp.bfloat16)
    zero = jnp.zeros_like(both)
    return jnp.concatenate(
        [jnp.where(first_tile == pair * 2, both, zero) for pair in range(TS // 16)], axis=0
    )


def tile_of(first):
    sub = lax.broadcasted_iota(jnp.int32, (8, TS), 0)
    tile = lax.shift_right_logical(first + ((sub - first) & 7), 3)
    return jnp.concatenate([tile, tile - 1], axis=0).astype(jnp.float32).astype(jnp.bfloat16)


def block_tile(halves):
    v_parts, w_parts = [], []
    for u_two, v_two, own in halves:
        u_first = jnp.broadcast_to(own[4:5], (8, TS)).astype(jnp.int32)
        v_first = jnp.broadcast_to(own[5:6], (8, TS)).astype(jnp.int32)
        u_tile, v_tile = tile_of(u_first), tile_of(v_first)
        for chan in range(2):
            v_parts.append(spread(turned(v_two[8 * chan:8 * chan + 8], v_first), v_tile))
            u_turned = turned(u_two[8 * chan:8 * chan + 8], u_first)
            w_parts.append(jnp.concatenate(
                [spread(u_turned * own[2 * chan + part:2 * chan + part + 1], u_tile) for part in range(2)],
                axis=0,
            ))
    return dot_rows(jnp.concatenate(w_parts, axis=1), jnp.concatenate(v_parts, axis=1))


def dot_rows(left, right):
    return lax.dot_general(left, right, (((1,), (1,)), ((), ())), preferred_element_type=jnp.float32)


def start_all(pairs, sems):
    copies = [pltpu.make_async_copy(source, target, sems.at[turn]) for turn, (source, target) in enumerate(pairs)]
    for copy in copies:
        copy.start()
    return copies


def clear_counts(count, bands):
    def clear(owner, _):
        count[owner] = 0
        return 0

    lax.fori_loop(0, bands, clear, 0)


def overflow_mark(route, count):
    mark = jnp.int32(0)
    for block in range(NB):
        owner = route[block]
        seen = count[owner]
        count[owner] = seen + 1
        mark = jnp.where(seen == DIRECT, jnp.where(mark == 0, owner + 1, MANY), mark)
    return mark


def pack_kernel(
    bands, shared,
    route_hbm, slot_hbm, u_hbm, v_hbm, vis_hbm, uo_hbm, vo_hbm, out_ref,
    route, slot, u_ref, v_ref, vis_ref, uo_ref, vo_ref, count, sems,
):
    copies = start_all(
        (
            (route_hbm, route), (slot_hbm, slot), (u_hbm, u_ref), (v_hbm, v_ref),
            (vis_hbm, vis_ref), (uo_hbm, uo_ref), (vo_hbm, vo_ref),
        ),
        sems,
    )
    per_owner = DIRECT * TILES
    clear_counts(count, bands)
    copies[0].wait()
    copies[1].wait()
    mark = jnp.int32(0)
    if shared:
        mark = overflow_mark(route, count)
        clear_counts(count, bands)
    marks = jnp.broadcast_to(mark, (1, TS)).astype(jnp.float32)
    nothing = jnp.zeros((7, TS), jnp.float32)
    blank = jnp.concatenate([nothing, marks, nothing, marks], axis=0).astype(jnp.bfloat16)
    empty = jnp.zeros((16, TS), jnp.bfloat16)
    for target in range(bands * DIRECT):
        for tile in range(TILES - 1):
            out_ref[target * TILES + tile] = empty
        out_ref[target * TILES + TILES - 1] = blank
    for copy in copies[2:]:
        copy.wait()

    for block in range(NB):
        owner = route[block]
        rank = count[owner]
        count[owner] = rank + 1
        base = owner * per_owner + rank * TILES

        @pl.when((owner + 1 != mark) & (rank < DIRECT))
        def _():
            place = jnp.full((1, TS), slot[block] + 1, jnp.int32).astype(jnp.float32)
            misc = []
            for half in range(2):
                lanes = slice(block * BLOCK + half * TS, block * BLOCK + half * TS + TS)
                row = block * 2 + half
                out_ref[base + half] = u_ref[:, lanes]
                out_ref[base + 2 + half] = v_ref[:, lanes]
                misc += [
                    vis_ref[0, :, lanes].astype(jnp.float32),
                    vis_ref[1, :, lanes].astype(jnp.float32),
                    uo_ref[row:row + 1, :].astype(jnp.float32),
                    vo_ref[row:row + 1, :].astype(jnp.float32),
                    place,
                    marks,
                ]
            out_ref[base + 4] = jnp.concatenate(misc, axis=0).astype(jnp.bfloat16)


def own_kernel(
    bands,
    route_hbm, slot_hbm, u_hbm, v_hbm, vis_hbm, uo_hbm, vo_hbm, table_hbm, share_0, share_1, share_2, share_3,
    route, slot, u_ref, v_ref, vis_ref, uo_ref, vo_ref, count, sems, listed, grid, table, table_sem,
):
    copies = start_all(
        (
            (route_hbm, route), (slot_hbm, slot), (u_hbm, u_ref), (v_hbm, v_ref),
            (vis_hbm, vis_ref), (uo_hbm, uo_ref), (vo_hbm, vo_ref),
        ),
        sems,
    )
    table_copy = pltpu.make_async_copy(table_hbm, table, table_sem)
    table_copy.start()
    grid[...] = jnp.zeros_like(grid)
    clear_counts(count, bands)
    copies[0].wait()
    copies[1].wait()
    mark = overflow_mark(route, count)
    filled = jnp.int32(0)
    for block in range(NB):
        listed[filled] = block
        filled = filled + (route[block] + 1 == mark).astype(jnp.int32)
    for copy in copies[2:]:
        copy.wait()

    def own_tile(block, used):
        halves = []
        for half in range(2):
            lanes = pl.ds(pl.multiple_of(block * BLOCK + half * TS, TS), TS)
            row = pl.ds(block * 2 + half, 1)
            own = jnp.concatenate(
                [
                    vis_ref[0, :, lanes].astype(jnp.float32) * used,
                    vis_ref[1, :, lanes].astype(jnp.float32) * used,
                    uo_ref[row, :].astype(jnp.float32),
                    vo_ref[row, :].astype(jnp.float32),
                ],
                axis=0,
            )
            halves.append((u_ref[:, lanes].astype(jnp.float32), v_ref[:, lanes].astype(jnp.float32), own))
        return block_tile(halves)

    def add_blocks(turn, _):
        for lane in range(4):
            number = turn * 4 + lane
            block = listed[jnp.minimum(number, filled - 1)]
            cells = pl.ds(pl.multiple_of(slot[block] * TS, TS), TS)
            grid[:, cells] += own_tile(block, (number < filled).astype(jnp.float32))
        return 0

    lax.fori_loop(0, (filled + 3) // 4, add_blocks, 0)
    me = lax.axis_index("tile") % PEERS
    width = TS // PEERS
    shares = (share_0, share_1, share_2, share_3)
    plain, turned_over = [], []
    for turn in range(PEERS):
        first = pl.multiple_of((me ^ turn) * width, width)
        real, imag = [grid[pl.ds(part * TS + first, width), :].astype(jnp.bfloat16) for part in range(2)]
        plain += [real, imag]
        turned_over += [-imag, real]
    both = jnp.concatenate([jnp.concatenate(plain, axis=0), jnp.concatenate(turned_over, axis=0)], axis=1)
    rows = IMY // share_0.shape[0]
    step = 256
    table_copy.wait()
    for first in range(0, IMY, step):
        part = dot_rows(table[first:first + step, :], both).astype(jnp.bfloat16)
        for row in range(0, step, rows):
            middle = row + rows // 2
            for turn, share_ref in enumerate(shares):
                lanes = slice(2 * width * turn, 2 * width * (turn + 1))
                pieces = [part[row:middle, lanes], part[middle:row + rows, lanes]]
                share_ref[(first + row) // rows] = jnp.concatenate(pieces, axis=1)


def hold_kernel(flags, table_hbm, *refs):
    parts, own, sems = refs[:-2], refs[-2], refs[-1]
    rows = parts[0].shape[0]
    pairs = [(table_hbm.at[pl.ds(turn * rows, rows), :], part) for turn, part in enumerate(parts)]
    width = TS // PEERS
    for turn in range(2 * PEERS):
        peer, part = turn // 2, turn % 2
        first = pl.multiple_of((flags[1] * 2 + part) * TS + peer * width, width)
        pairs.append((table_hbm.at[pl.ds(first, width), :], own.at[pl.ds(turn * width, width), :]))
    for copy in start_all(pairs, sems):
        copy.wait()


def got_tile(got_ref, base):
    misc = got_ref[base + 4].astype(jnp.float32)
    halves = [
        (got_ref[base + half].astype(jnp.float32), got_ref[base + 2 + half].astype(jnp.float32), misc[8 * half:8 * half + 8])
        for half in range(2)
    ]
    return misc, block_tile(halves)


def turned_parts(rounded):
    half = rounded.shape[0] // 2
    return jnp.concatenate([rounded, jnp.concatenate([-rounded[half:], rounded[:half]], axis=0)], axis=1)


def write_columns(grid, table, out_ref):
    both = turned_parts(grid[...].astype(jnp.bfloat16))
    rows = IMY // out_ref.shape[0]
    step = 256
    for first in range(0, IMY, step):
        part = dot_rows(table[first:first + step, :], both)
        for row in range(0, step, rows):
            pieces = [part[row:row + rows, :TS], part[row:row + rows, TS:]]
            out_ref[(first + row) // rows, :2 * rows, :] = jnp.concatenate(pieces, axis=0).astype(jnp.bfloat16)


def full_grid_kernel(places, got_ref, table_hbm, out_ref, grid, table, sem):
    copy = pltpu.make_async_copy(table_hbm, table, sem)
    copy.start()
    grid[...] = jnp.zeros_like(grid)
    tiles = got_ref.shape[0]

    def add_slot(index, _):
        @pl.when(places[index] > 0)
        def _():
            cells = pl.ds(pl.multiple_of((places[index] - 1) * TS, TS), TS)
            grid[:, cells] += got_tile(got_ref, index * TILES)[1]

        return 0

    lax.fori_loop(0, tiles // TILES, add_slot, 0)
    out_ref[...] = jnp.zeros_like(out_ref)
    copy.wait()
    write_columns(grid, table, out_ref)


def grid_kernel(bands, shared, got_ref, *refs):
    shares = refs[:PEERS] if shared else ()
    table_hbm, out_ref, flags, grid, table, sem = refs[len(shares):]
    copy = pltpu.make_async_copy(table_hbm, table, sem)
    copy.start()
    grid[...] = jnp.zeros_like(grid)
    per_owner = DIRECT * TILES

    def add_source(source, carried):
        least, most = carried
        for rank in range(DIRECT):
            misc, tile = got_tile(got_ref, source * per_owner + rank * TILES)
            place = jnp.maximum(misc[6, 0].astype(jnp.int32) - 1, 0)
            cells = pl.ds(pl.multiple_of(place * TS, TS), TS)
            grid[:, cells] += tile
        marks = misc[:8]
        return jnp.minimum(least, jnp.where(marks == 0.0, float(MANY), marks)), jnp.maximum(most, marks)

    start = (jnp.full((8, TS), float(MANY), jnp.float32), jnp.zeros((8, TS), jnp.float32))
    least, most = lax.fori_loop(0, bands, add_source, start, unroll=8)
    low, high = least[7, 0].astype(jnp.int32), most[7, 0].astype(jnp.int32)
    flags[0] = ((high == 0) | ((low == high) & (high != MANY))).astype(jnp.int32)
    flags[1] = jnp.where(high == MANY, 0, jnp.maximum(high - 1, 0))
    if shared:
        own = shares[0][...].astype(jnp.float32)
        for share in shares[1:]:
            own += share[...].astype(jnp.float32)
        out_ref[:, out_ref.shape[1] - 16:, :] = own.astype(jnp.bfloat16)
    copy.wait()
    write_columns(grid, table, out_ref)


def side_by_side(got_ref, band, group, first, rows):
    return jnp.concatenate(
        [got_ref[band, group, first:first + rows, :], got_ref[band, group, first + rows:first + 2 * rows, :]], axis=1
    )


def band_dot(got_ref, table, rows, bands):
    left = jnp.concatenate(
        [
            jnp.concatenate([side_by_side(got_ref, band, group, 0, rows) for band in bands], axis=1)
            for group in range(got_ref.shape[1])
        ],
        axis=0,
    )
    return jnp.dot(left, table, preferred_element_type=jnp.float32)


def image_kernel(scale, got_ref, *refs):
    held = refs[:HELD]
    own_ref, table_hbm, out_ref, table_ref, sems = refs[HELD:]
    rows = out_ref.shape[0]
    bands, groups = got_ref.shape[:2]
    pairs = []
    for band in range(HELD, bands):
        lines = pl.ds(band * 2 * TS, 2 * TS)
        pairs.append((table_hbm.at[lines, :], table_ref.at[pl.ds((band - HELD) * 2 * TS, 2 * TS), :]))
    copies = start_all(pairs, sems)
    width = TS // PEERS
    left = []
    for peer in range(PEERS):
        per_group = []
        for group in range(groups):
            added = got_ref[peer, group, 2 * rows:, :].astype(jnp.float32)
            for band in range(peer + PEERS, bands, PEERS):
                added += got_ref[band, group, 2 * rows:, :].astype(jnp.float32)
            per_group += [added[:, :2 * width], added[:, 2 * width:]]
        left.append(jnp.concatenate(per_group, axis=0))
    total = jnp.dot(
        jnp.concatenate(left, axis=1).astype(jnp.bfloat16), own_ref[...], preferred_element_type=jnp.float32
    )
    table = jnp.concatenate([part[...] for part in held], axis=0)
    total = total + band_dot(got_ref, table, rows, range(HELD))
    for first in range(HELD, bands, HELD):
        for band in range(first, first + HELD):
            copies[band - HELD].wait()
        table = table_ref[(first - HELD) * 2 * TS:first * 2 * TS, :]
        total = total + band_dot(got_ref, table, rows, range(first, first + HELD))
    image = total[:rows]
    for group in range(1, groups):
        image = image + total[group * rows:(group + 1) * rows]
    out_ref[...] = image * scale


def plain_image_kernel(scale, got_ref, table_ref, out_ref, total):
    turn = pl.program_id(0)

    @pl.when(turn == 0)
    def _():
        total[...] = jnp.zeros_like(total)

    rows = out_ref.shape[0]
    part = total[...] + band_dot(got_ref, table_ref[...], rows, range(got_ref.shape[0]))
    total[...] = part

    @pl.when(turn == pl.num_programs(0) - 1)
    def _():
        out_ref[...] = (part[:rows] + part[rows:]) * scale


VMEM = pl.BlockSpec(memory_space=pltpu.VMEM)
SMEM = pl.BlockSpec(memory_space=pltpu.SMEM)
HBM = pl.BlockSpec(memory_space=pltpu.HBM)
PARAMS = pltpu.CompilerParams(vmem_limit_bytes=20 * 1024 * 1024)


def body(visibility, u_kernel, v_kernel, u_offset, v_offset, tile_route, tile_slot):
    bands = lax.axis_size("tile")
    groups = lax.axis_size("chan")
    local_rows = visibility.shape[2]
    capacity = 4 * NB // bands
    shared = capacity > DIRECT
    rows_y = IMY // (bands * groups)
    sent_rows = 2 * rows_y + (16 if shared else 0)
    columns_shape = jax.ShapeDtypeStruct((bands * groups, sent_rows, TS), jnp.bfloat16)
    v_table = jnp.asarray(column_table())
    operands = (
        tile_route[:, 0],
        tile_slot,
        u_kernel.reshape(2 * KS, local_rows),
        v_kernel.reshape(2 * KS, local_rows),
        visibility,
        u_offset.reshape(NB * 2, TS),
        v_offset.reshape(NB * 2, TS),
    )
    grid_scratch = [
        pltpu.VMEM((2 * TS, TPD * TS), jnp.float32),
        pltpu.VMEM((IMY, 2 * TPD * TS), jnp.bfloat16),
        pltpu.SemaphoreType.DMA,
    ]
    raw_scratch = [
        pltpu.SMEM((NB,), jnp.int32),
        pltpu.SMEM((NB,), jnp.int32),
        pltpu.VMEM((2 * KS, local_rows), jnp.bfloat16),
        pltpu.VMEM((2 * KS, local_rows), jnp.bfloat16),
        pltpu.VMEM(visibility.shape, jnp.bfloat16),
        pltpu.VMEM((NB * 2, TS), jnp.int32),
        pltpu.VMEM((NB * 2, TS), jnp.int32),
    ]
    raw_scratch += [pltpu.SMEM((bands,), jnp.int32), pltpu.SemaphoreType.DMA((7,))]
    packed = pl.pallas_call(
        functools.partial(pack_kernel, bands, shared),
        out_shape=jax.ShapeDtypeStruct((bands * DIRECT * TILES, 16, TS), jnp.bfloat16),
        in_specs=[HBM] * 7,
        out_specs=VMEM,
        scratch_shapes=raw_scratch,
        compiler_params=PARAMS,
    )(*operands)
    got = lax.all_to_all(packed, "tile", split_axis=0, concat_axis=0, tiled=True)
    u_table = jnp.asarray(image_table(bands))
    partial = ()
    if shared:
        own = pl.pallas_call(
            functools.partial(own_kernel, bands),
            out_shape=[jax.ShapeDtypeStruct((bands * groups, 16, TS), jnp.bfloat16)] * PEERS,
            in_specs=[HBM] * 8,
            out_specs=[VMEM] * PEERS,
            scratch_shapes=raw_scratch + [
                pltpu.SMEM((NB + 1,), jnp.int32), pltpu.VMEM((2 * TS, TPD * TS), jnp.float32),
                pltpu.VMEM((IMY, 2 * TPD * TS), jnp.bfloat16), pltpu.SemaphoreType.DMA,
            ],
            compiler_params=PARAMS,
            cost_estimate=pl.CostEstimate(flops=10 ** 9, bytes_accessed=6 * 10 ** 6, transcendentals=0),
        )(*operands, v_table)
        summed = [own[0]] + [
            lax.ppermute(own[turn], "tile", [(band, band ^ turn) for band in range(bands)]) for turn in (3, 1, 2)
        ]
        partial = tuple(summed)
    columns, flags = pl.pallas_call(
        functools.partial(grid_kernel, bands, shared),
        out_shape=(columns_shape, jax.ShapeDtypeStruct((2,), jnp.int32)),
        in_specs=[VMEM] * (1 + len(partial)) + [HBM],
        out_specs=(VMEM, SMEM),
        scratch_shapes=grid_scratch,
        compiler_params=PARAMS,
    )(got, *partial, v_table)

    scale = 1.0 / (KS * KS * math.sqrt(local_rows * bands * CH))
    image_shape = jax.ShapeDtypeStruct((rows_y, IMX), jnp.float32)

    def exchanged(columns):
        sent = lax.all_to_all(columns, ("tile", "chan"), split_axis=0, concat_axis=0, tiled=True)
        return sent.reshape(bands, groups, sent_rows, TS)

    def plain_image(columns):
        per_turn = 4
        return pl.pallas_call(
            functools.partial(plain_image_kernel, scale),
            out_shape=image_shape,
            grid=(bands // per_turn,),
            in_specs=[
                pl.BlockSpec((per_turn, groups, sent_rows, TS), lambda turn: (turn, 0, 0, 0)),
                pl.BlockSpec((per_turn * 2 * TS, IMX), lambda turn: (turn, 0)),
            ],
            out_specs=pl.BlockSpec((rows_y, IMX), lambda turn: (0, 0)),
            scratch_shapes=[pltpu.VMEM((groups * rows_y, IMX), jnp.float32)],
            compiler_params=PARAMS,
        )(exchanged(columns), u_table)

    if not shared:
        return plain_image(columns)

    def every_slot(_):
        slots = bands * capacity
        packed = pl.pallas_call(
            functools.partial(full_pack_kernel, capacity),
            out_shape=jax.ShapeDtypeStruct((slots * TILES, 16, TS), jnp.bfloat16),
            in_specs=[SMEM, SMEM, VMEM, VMEM, VMEM, VMEM, VMEM],
            out_specs=VMEM,
            scratch_shapes=[pltpu.SMEM((bands,), jnp.int32)],
            compiler_params=PARAMS,
        )(*operands)
        got = lax.all_to_all(packed, "tile", split_axis=0, concat_axis=0, tiled=True)
        places = got.reshape(slots, TILES, 16, TS)[:, TILES - 1, 6, 0].astype(jnp.int32)
        columns = pl.pallas_call(
            full_grid_kernel,
            out_shape=columns_shape,
            in_specs=[SMEM, VMEM, HBM],
            out_specs=VMEM,
            scratch_shapes=grid_scratch,
            compiler_params=PARAMS,
        )(places, got, v_table)
        return plain_image(columns)

    held = pl.pallas_call(
        hold_kernel,
        out_shape=[jax.ShapeDtypeStruct((2 * TS, IMX), jnp.bfloat16)] * HELD
        + [jax.ShapeDtypeStruct((2 * TS, IMX), jnp.bfloat16)],
        in_specs=[SMEM, HBM],
        out_specs=[VMEM] * (HELD + 1),
        scratch_shapes=[pltpu.SemaphoreType.DMA((HELD + 2 * PEERS,))],
        compiler_params=PARAMS,
        cost_estimate=pl.CostEstimate(flops=0, bytes_accessed=16 * 10 ** 6, transcendentals=0),
    )(flags, u_table)
    image = pl.pallas_call(
        functools.partial(image_kernel, scale),
        out_shape=image_shape,
        in_specs=[VMEM] * (HELD + 2) + [HBM],
        out_specs=VMEM,
        scratch_shapes=[
            pltpu.VMEM(((bands - HELD) * 2 * TS, IMX), jnp.bfloat16),
            pltpu.SemaphoreType.DMA((bands - HELD,)),
        ],
        compiler_params=PARAMS,
    )(exchanged(columns), *held, u_table)
    return lax.cond(flags[0] == 1, lambda kept: kept, every_slot, image)


def solution(mesh):
    placed = (
        P("chan", None, "tile"),
        P("chan", None, "tile"),
        P("chan", None, "tile"),
        P("tile"),
        P("tile"),
        P("tile", None),
        P("tile"),
    )
    return jax.shard_map(
        body, mesh=mesh, in_specs=placed, out_specs=P(("tile", "chan"), None), check_vma=False
    )
```

```python
import functools
import math

import jax
import jax.numpy as jnp
import ml_dtypes
import numpy as np
from jax import lax
from jax.experimental import pallas as pl
from jax.experimental.pallas import tpu as pltpu
from jax.sharding import PartitionSpec as P

NG = 16384
CH = 4
KS = 8
BLOCK = 256
TS = 128
TPD = 8
NB = 32
IMX = 1024
IMY = 1024
ROWS = 80
TILES = ROWS // 16
DIRECT = 2
HELD = 4
PEERS = 4
MANY = 255


def phase_table(rows_coord, cols_coord):
    turns = np.mod(rows_coord[:, None].astype(np.int64) * cols_coord[None, :].astype(np.int64), NG)
    angles = turns.astype(np.float64) * (2.0 * math.pi / NG)
    return np.cos(angles).astype(ml_dtypes.bfloat16), np.sin(angles).astype(ml_dtypes.bfloat16)


def column_table():
    cos_v, sin_v = phase_table(np.arange(IMY) - IMY // 2, np.arange(TPD * TS))
    return np.concatenate([cos_v, sin_v], axis=1)


def image_table(bands):
    cos_u, sin_u = phase_table(np.arange(bands * TS), np.arange(IMX) - IMX // 2)
    both = np.stack([cos_u.reshape(bands, TS, IMX), (-sin_u).reshape(bands, TS, IMX)], axis=1)
    return both.reshape(bands * 2 * TS, IMX)


def full_pack_kernel(
    capacity,
    route_hbm, slot_hbm, u_hbm, v_hbm, vis_hbm, uo_hbm, vo_hbm, out_ref,
    route, slot, u_ref, v_ref, vis_ref, uo_ref, vo_ref, count, sems,
):
    copies = start_all(
        (
            (route_hbm, route), (slot_hbm, slot), (u_hbm, u_ref), (v_hbm, v_ref),
            (vis_hbm, vis_ref), (uo_hbm, uo_ref), (vo_hbm, vo_ref),
        ),
        sems,
    )
    for copy in copies:
        copy.wait()
    owners = out_ref.shape[0] // (capacity * TILES)
    out_ref[...] = jnp.zeros_like(out_ref)

    def clear(owner, _):
        count[owner] = 0
        return 0

    lax.fori_loop(0, owners, clear, 0)
    for block in range(NB):
        owner = route[block]
        rank = count[owner]
        count[owner] = rank + 1
        base = (owner * capacity + rank) * TILES
        place = jnp.full((1, TS), slot[block] + 1, jnp.int32).astype(jnp.float32)
        misc = []
        for half in range(2):
            lanes = slice(block * BLOCK + half * TS, block * BLOCK + half * TS + TS)
            row = block * 2 + half
            out_ref[base + half] = u_ref[:, lanes]
            out_ref[base + 2 + half] = v_ref[:, lanes]
            misc += [
                vis_ref[0, :, lanes].astype(jnp.float32),
                vis_ref[1, :, lanes].astype(jnp.float32),
                uo_ref[row:row + 1, :].astype(jnp.float32),
                vo_ref[row:row + 1, :].astype(jnp.float32),
                place,
                jnp.zeros((1, TS), jnp.float32),
            ]
        out_ref[base + 4] = jnp.concatenate(misc, axis=0).astype(jnp.bfloat16)


def turned(kernel, first):
    for bit in (1, 2, 4):
        kernel = jnp.where((first & bit) != 0, pltpu.roll(kernel, bit, 0), kernel)
    return kernel


def spread(kernel, first_tile):
    both = jnp.concatenate([kernel, kernel], axis=0).astype(jnp.bfloat16)
    zero = jnp.zeros_like(both)
    return jnp.concatenate(
        [jnp.where(first_tile == pair * 2, both, zero) for pair in range(TS // 16)], axis=0
    )


def tile_of(first):
    sub = lax.broadcasted_iota(jnp.int32, (8, TS), 0)
    tile = lax.shift_right_logical(first + ((sub - first) & 7), 3)
    return jnp.concatenate([tile, tile - 1], axis=0).astype(jnp.float32).astype(jnp.bfloat16)


def block_tile(halves):
    v_parts, w_parts = [], []
    for u_two, v_two, own in halves:
        u_first = jnp.broadcast_to(own[4:5], (8, TS)).astype(jnp.int32)
        v_first = jnp.broadcast_to(own[5:6], (8, TS)).astype(jnp.int32)
        u_tile, v_tile = tile_of(u_first), tile_of(v_first)
        for chan in range(2):
            v_parts.append(spread(turned(v_two[8 * chan:8 * chan + 8], v_first), v_tile))
            u_turned = turned(u_two[8 * chan:8 * chan + 8], u_first)
            w_parts.append(jnp.concatenate(
                [spread(u_turned * own[2 * chan + part:2 * chan + part + 1], u_tile) for part in range(2)],
                axis=0,
            ))
    return dot_rows(jnp.concatenate(w_parts, axis=1), jnp.concatenate(v_parts, axis=1))


def dot_rows(left, right):
    return lax.dot_general(left, right, (((1,), (1,)), ((), ())), preferred_element_type=jnp.float32)


def start_all(pairs, sems):
    copies = [pltpu.make_async_copy(source, target, sems.at[turn]) for turn, (source, target) in enumerate(pairs)]
    for copy in copies:
        copy.start()
    return copies


def clear_counts(count, bands):
    def clear(owner, _):
        count[owner] = 0
        return 0

    lax.fori_loop(0, bands, clear, 0)


def overflow_mark(route, count):
    mark = jnp.int32(0)
    for block in range(NB):
        owner = route[block]
        seen = count[owner]
        count[owner] = seen + 1
        mark = jnp.where(seen == DIRECT, jnp.where(mark == 0, owner + 1, MANY), mark)
    return mark


def pack_kernel(
    bands, shared,
    route_hbm, slot_hbm, u_hbm, v_hbm, vis_hbm, uo_hbm, vo_hbm, out_ref,
    route, slot, u_ref, v_ref, vis_ref, uo_ref, vo_ref, count, sems,
):
    copies = start_all(
        (
            (route_hbm, route), (slot_hbm, slot), (u_hbm, u_ref), (v_hbm, v_ref),
            (vis_hbm, vis_ref), (uo_hbm, uo_ref), (vo_hbm, vo_ref),
        ),
        sems,
    )
    per_owner = DIRECT * TILES
    clear_counts(count, bands)
    copies[0].wait()
    copies[1].wait()
    mark = jnp.int32(0)
    if shared:
        mark = overflow_mark(route, count)
        clear_counts(count, bands)
    marks = jnp.broadcast_to(mark, (1, TS)).astype(jnp.float32)
    nothing = jnp.zeros((7, TS), jnp.float32)
    blank = jnp.concatenate([nothing, marks, nothing, marks], axis=0).astype(jnp.bfloat16)
    empty = jnp.zeros((16, TS), jnp.bfloat16)
    for target in range(bands * DIRECT):
        for tile in range(TILES - 1):
            out_ref[target * TILES + tile] = empty
        out_ref[target * TILES + TILES - 1] = blank
    for copy in copies[2:]:
        copy.wait()

    for block in range(NB):
        owner = route[block]
        rank = count[owner]
        count[owner] = rank + 1
        base = owner * per_owner + rank * TILES

        @pl.when((owner + 1 != mark) & (rank < DIRECT))
        def _():
            place = jnp.full((1, TS), slot[block] + 1, jnp.int32).astype(jnp.float32)
            misc = []
            for half in range(2):
                lanes = slice(block * BLOCK + half * TS, block * BLOCK + half * TS + TS)
                row = block * 2 + half
                out_ref[base + half] = u_ref[:, lanes]
                out_ref[base + 2 + half] = v_ref[:, lanes]
                misc += [
                    vis_ref[0, :, lanes].astype(jnp.float32),
                    vis_ref[1, :, lanes].astype(jnp.float32),
                    uo_ref[row:row + 1, :].astype(jnp.float32),
                    vo_ref[row:row + 1, :].astype(jnp.float32),
                    place,
                    marks,
                ]
            out_ref[base + 4] = jnp.concatenate(misc, axis=0).astype(jnp.bfloat16)


def own_kernel(
    bands,
    route_hbm, slot_hbm, u_hbm, v_hbm, vis_hbm, uo_hbm, vo_hbm, table_hbm, share_0, share_1, share_2, share_3,
    route, slot, u_ref, v_ref, vis_ref, uo_ref, vo_ref, count, sems, listed, grid, table, table_sem,
):
    copies = start_all(
        (
            (route_hbm, route), (slot_hbm, slot), (u_hbm, u_ref), (v_hbm, v_ref),
            (vis_hbm, vis_ref), (uo_hbm, uo_ref), (vo_hbm, vo_ref),
        ),
        sems,
    )
    table_copy = pltpu.make_async_copy(table_hbm, table, table_sem)
    table_copy.start()
    grid[...] = jnp.zeros_like(grid)
    clear_counts(count, bands)
    copies[0].wait()
    copies[1].wait()
    mark = overflow_mark(route, count)
    filled = jnp.int32(0)
    for block in range(NB):
        listed[filled] = block
        filled = filled + (route[block] + 1 == mark).astype(jnp.int32)
    for copy in copies[2:]:
        copy.wait()

    def own_tile(block, used):
        halves = []
        for half in range(2):
            lanes = pl.ds(pl.multiple_of(block * BLOCK + half * TS, TS), TS)
            row = pl.ds(block * 2 + half, 1)
            own = jnp.concatenate(
                [
                    vis_ref[0, :, lanes].astype(jnp.float32) * used,
                    vis_ref[1, :, lanes].astype(jnp.float32) * used,
                    uo_ref[row, :].astype(jnp.float32),
                    vo_ref[row, :].astype(jnp.float32),
                ],
                axis=0,
            )
            halves.append((u_ref[:, lanes].astype(jnp.float32), v_ref[:, lanes].astype(jnp.float32), own))
        return block_tile(halves)

    def add_blocks(turn, _):
        for lane in range(4):
            number = turn * 4 + lane
            block = listed[jnp.minimum(number, filled - 1)]
            cells = pl.ds(pl.multiple_of(slot[block] * TS, TS), TS)
            grid[:, cells] += own_tile(block, (number < filled).astype(jnp.float32))
        return 0

    lax.fori_loop(0, (filled + 3) // 4, add_blocks, 0)
    me = lax.axis_index("tile") % PEERS
    width = TS // PEERS
    shares = (share_0, share_1, share_2, share_3)
    plain, turned_over = [], []
    for turn in range(PEERS):
        first = pl.multiple_of((me ^ turn) * width, width)
        real, imag = [grid[pl.ds(part * TS + first, width), :].astype(jnp.bfloat16) for part in range(2)]
        plain += [real, imag]
        turned_over += [-imag, real]
    both = jnp.concatenate([jnp.concatenate(plain, axis=0), jnp.concatenate(turned_over, axis=0)], axis=1)
    rows = IMY // share_0.shape[0]
    step = 256
    table_copy.wait()
    for first in range(0, IMY, step):
        part = dot_rows(table[first:first + step, :], both).astype(jnp.bfloat16)
        for row in range(0, step, rows):
            middle = row + rows // 2
            for turn, share_ref in enumerate(shares):
                lanes = slice(2 * width * turn, 2 * width * (turn + 1))
                pieces = [part[row:middle, lanes], part[middle:row + rows, lanes]]
                share_ref[(first + row) // rows] = jnp.concatenate(pieces, axis=1)


def hold_kernel(flags, table_hbm, *refs):
    parts, own, sems = refs[:-2], refs[-2], refs[-1]
    rows = parts[0].shape[0]
    pairs = [(table_hbm.at[pl.ds(turn * rows, rows), :], part) for turn, part in enumerate(parts)]
    width = TS // PEERS
    for turn in range(2 * PEERS):
        peer, part = turn // 2, turn % 2
        first = pl.multiple_of((flags[1] * 2 + part) * TS + peer * width, width)
        pairs.append((table_hbm.at[pl.ds(first, width), :], own.at[pl.ds(turn * width, width), :]))
    for copy in start_all(pairs, sems):
        copy.wait()


def got_tile(got_ref, base):
    misc = got_ref[base + 4].astype(jnp.float32)
    halves = [
        (got_ref[base + half].astype(jnp.float32), got_ref[base + 2 + half].astype(jnp.float32), misc[8 * half:8 * half + 8])
        for half in range(2)
    ]
    return misc, block_tile(halves)


def turned_parts(rounded):
    half = rounded.shape[0] // 2
    return jnp.concatenate([rounded, jnp.concatenate([-rounded[half:], rounded[:half]], axis=0)], axis=1)


def write_columns(grid, table, out_ref):
    both = turned_parts(grid[...].astype(jnp.bfloat16))
    rows = IMY // out_ref.shape[0]
    step = 256
    for first in range(0, IMY, step):
        part = dot_rows(table[first:first + step, :], both)
        for row in range(0, step, rows):
            pieces = [part[row:row + rows, :TS], part[row:row + rows, TS:]]
            out_ref[(first + row) // rows, :2 * rows, :] = jnp.concatenate(pieces, axis=0).astype(jnp.bfloat16)


def full_grid_kernel(places, got_ref, table_hbm, out_ref, grid, table, sem):
    copy = pltpu.make_async_copy(table_hbm, table, sem)
    copy.start()
    grid[...] = jnp.zeros_like(grid)
    tiles = got_ref.shape[0]

    def add_slot(index, _):
        @pl.when(places[index] > 0)
        def _():
            cells = pl.ds(pl.multiple_of((places[index] - 1) * TS, TS), TS)
            grid[:, cells] += got_tile(got_ref, index * TILES)[1]

        return 0

    lax.fori_loop(0, tiles // TILES, add_slot, 0)
    out_ref[...] = jnp.zeros_like(out_ref)
    copy.wait()
    write_columns(grid, table, out_ref)


def grid_kernel(bands, shared, got_ref, *refs):
    shares = refs[:PEERS] if shared else ()
    table_hbm, out_ref, flags, grid, table, sem = refs[len(shares):]
    copy = pltpu.make_async_copy(table_hbm, table, sem)
    copy.start()
    grid[...] = jnp.zeros_like(grid)
    per_owner = DIRECT * TILES

    def add_source(source, carried):
        least, most = carried
        for rank in range(DIRECT):
            misc, tile = got_tile(got_ref, source * per_owner + rank * TILES)
            place = jnp.maximum(misc[6, 0].astype(jnp.int32) - 1, 0)
            cells = pl.ds(pl.multiple_of(place * TS, TS), TS)
            grid[:, cells] += tile
        marks = misc[:8]
        return jnp.minimum(least, jnp.where(marks == 0.0, float(MANY), marks)), jnp.maximum(most, marks)

    start = (jnp.full((8, TS), float(MANY), jnp.float32), jnp.zeros((8, TS), jnp.float32))
    least, most = lax.fori_loop(0, bands, add_source, start, unroll=8)
    low, high = least[7, 0].astype(jnp.int32), most[7, 0].astype(jnp.int32)
    flags[0] = ((high == 0) | ((low == high) & (high != MANY))).astype(jnp.int32)
    flags[1] = jnp.where(high == MANY, 0, jnp.maximum(high - 1, 0))
    if shared:
        own = shares[0][...].astype(jnp.float32)
        for share in shares[1:]:
            own += share[...].astype(jnp.float32)
        out_ref[:, out_ref.shape[1] - 16:, :] = own.astype(jnp.bfloat16)
    copy.wait()
    write_columns(grid, table, out_ref)


def side_by_side(got_ref, band, group, first, rows):
    return jnp.concatenate(
        [got_ref[band, group, first:first + rows, :], got_ref[band, group, first + rows:first + 2 * rows, :]], axis=1
    )


def band_dot(got_ref, table, rows, bands):
    left = jnp.concatenate(
        [
            jnp.concatenate([side_by_side(got_ref, band, group, 0, rows) for band in bands], axis=1)
            for group in range(got_ref.shape[1])
        ],
        axis=0,
    )
    return jnp.dot(left, table, preferred_element_type=jnp.float32)


def image_kernel(scale, got_ref, *refs):
    held = refs[:HELD]
    own_ref, table_hbm, out_ref, table_ref, sems = refs[HELD:]
    rows = out_ref.shape[0]
    bands, groups = got_ref.shape[:2]
    pairs = []
    for band in range(HELD, bands):
        lines = pl.ds(band * 2 * TS, 2 * TS)
        pairs.append((table_hbm.at[lines, :], table_ref.at[pl.ds((band - HELD) * 2 * TS, 2 * TS), :]))
    copies = start_all(pairs, sems)
    width = TS // PEERS
    left = []
    for peer in range(PEERS):
        per_group = []
        for group in range(groups):
            added = got_ref[peer, group, 2 * rows:, :].astype(jnp.float32)
            for band in range(peer + PEERS, bands, PEERS):
                added += got_ref[band, group, 2 * rows:, :].astype(jnp.float32)
            per_group += [added[:, :2 * width], added[:, 2 * width:]]
        left.append(jnp.concatenate(per_group, axis=0))
    total = jnp.dot(
        jnp.concatenate(left, axis=1).astype(jnp.bfloat16), own_ref[...], preferred_element_type=jnp.float32
    )
    table = jnp.concatenate([part[...] for part in held], axis=0)
    total = total + band_dot(got_ref, table, rows, range(HELD))
    for first in range(HELD, bands, HELD):
        for band in range(first, first + HELD):
            copies[band - HELD].wait()
        table = table_ref[(first - HELD) * 2 * TS:first * 2 * TS, :]
        total = total + band_dot(got_ref, table, rows, range(first, first + HELD))
    image = total[:rows]
    for group in range(1, groups):
        image = image + total[group * rows:(group + 1) * rows]
    out_ref[...] = image * scale


def plain_image_kernel(scale, got_ref, table_ref, out_ref, total):
    turn = pl.program_id(0)

    @pl.when(turn == 0)
    def _():
        total[...] = jnp.zeros_like(total)

    rows = out_ref.shape[0]
    part = total[...] + band_dot(got_ref, table_ref[...], rows, range(got_ref.shape[0]))
    total[...] = part

    @pl.when(turn == pl.num_programs(0) - 1)
    def _():
        out_ref[...] = (part[:rows] + part[rows:]) * scale


VMEM = pl.BlockSpec(memory_space=pltpu.VMEM)
SMEM = pl.BlockSpec(memory_space=pltpu.SMEM)
HBM = pl.BlockSpec(memory_space=pltpu.HBM)
PARAMS = pltpu.CompilerParams(vmem_limit_bytes=20 * 1024 * 1024)


def body(visibility, u_kernel, v_kernel, u_offset, v_offset, tile_route, tile_slot):
    bands = lax.axis_size("tile")
    groups = lax.axis_size("chan")
    local_rows = visibility.shape[2]
    capacity = 4 * NB // bands
    shared = capacity > DIRECT
    rows_y = IMY // (bands * groups)
    sent_rows = 2 * rows_y + (16 if shared else 0)
    columns_shape = jax.ShapeDtypeStruct((bands * groups, sent_rows, TS), jnp.bfloat16)
    v_table = jnp.asarray(column_table())
    operands = (
        tile_route[:, 0],
        tile_slot,
        u_kernel.reshape(2 * KS, local_rows),
        v_kernel.reshape(2 * KS, local_rows),
        visibility,
        u_offset.reshape(NB * 2, TS),
        v_offset.reshape(NB * 2, TS),
    )
    grid_scratch = [
        pltpu.VMEM((2 * TS, TPD * TS), jnp.float32),
        pltpu.VMEM((IMY, 2 * TPD * TS), jnp.bfloat16),
        pltpu.SemaphoreType.DMA,
    ]
    raw_scratch = [
        pltpu.SMEM((NB,), jnp.int32),
        pltpu.SMEM((NB,), jnp.int32),
        pltpu.VMEM((2 * KS, local_rows), jnp.bfloat16),
        pltpu.VMEM((2 * KS, local_rows), jnp.bfloat16),
        pltpu.VMEM(visibility.shape, jnp.bfloat16),
        pltpu.VMEM((NB * 2, TS), jnp.int32),
        pltpu.VMEM((NB * 2, TS), jnp.int32),
    ]
    raw_scratch += [pltpu.SMEM((bands,), jnp.int32), pltpu.SemaphoreType.DMA((7,))]
    packed = pl.pallas_call(
        functools.partial(pack_kernel, bands, shared),
        out_shape=jax.ShapeDtypeStruct((bands * DIRECT * TILES, 16, TS), jnp.bfloat16),
        in_specs=[HBM] * 7,
        out_specs=VMEM,
        scratch_shapes=raw_scratch,
        compiler_params=PARAMS,
    )(*operands)
    got = lax.all_to_all(packed, "tile", split_axis=0, concat_axis=0, tiled=True)
    u_table = jnp.asarray(image_table(bands))
    partial = ()
    if shared:
        own = pl.pallas_call(
            functools.partial(own_kernel, bands),
            out_shape=[jax.ShapeDtypeStruct((bands * groups, 16, TS), jnp.bfloat16)] * PEERS,
            in_specs=[HBM] * 8,
            out_specs=[VMEM] * PEERS,
            scratch_shapes=raw_scratch + [
                pltpu.SMEM((NB + 1,), jnp.int32), pltpu.VMEM((2 * TS, TPD * TS), jnp.float32),
                pltpu.VMEM((IMY, 2 * TPD * TS), jnp.bfloat16), pltpu.SemaphoreType.DMA,
            ],
            compiler_params=PARAMS,
            cost_estimate=pl.CostEstimate(flops=10 ** 9, bytes_accessed=6 * 10 ** 6, transcendentals=0),
        )(*operands, v_table)
        summed = [own[0]] + [
            lax.ppermute(own[turn], "tile", [(band, band ^ turn) for band in range(bands)]) for turn in (3, 1, 2)
        ]
        partial = tuple(summed)
    columns, flags = pl.pallas_call(
        functools.partial(grid_kernel, bands, shared),
        out_shape=(columns_shape, jax.ShapeDtypeStruct((2,), jnp.int32)),
        in_specs=[VMEM] * (1 + len(partial)) + [HBM],
        out_specs=(VMEM, SMEM),
        scratch_shapes=grid_scratch,
        compiler_params=PARAMS,
    )(got, *partial, v_table)

    scale = 1.0 / (KS * KS * math.sqrt(local_rows * bands * CH))
    image_shape = jax.ShapeDtypeStruct((rows_y, IMX), jnp.float32)

    def exchanged(columns):
        sent = lax.all_to_all(columns, ("tile", "chan"), split_axis=0, concat_axis=0, tiled=True)
        return sent.reshape(bands, groups, sent_rows, TS)

    def plain_image(columns):
        per_turn = 4
        return pl.pallas_call(
            functools.partial(plain_image_kernel, scale),
            out_shape=image_shape,
            grid=(bands // per_turn,),
            in_specs=[
                pl.BlockSpec((per_turn, groups, sent_rows, TS), lambda turn: (turn, 0, 0, 0)),
                pl.BlockSpec((per_turn * 2 * TS, IMX), lambda turn: (turn, 0)),
            ],
            out_specs=pl.BlockSpec((rows_y, IMX), lambda turn: (0, 0)),
            scratch_shapes=[pltpu.VMEM((groups * rows_y, IMX), jnp.float32)],
            compiler_params=PARAMS,
        )(exchanged(columns), u_table)

    if not shared:
        return plain_image(columns)

    def every_slot(_):
        slots = bands * capacity
        packed = pl.pallas_call(
            functools.partial(full_pack_kernel, capacity),
            out_shape=jax.ShapeDtypeStruct((slots * TILES, 16, TS), jnp.bfloat16),
            in_specs=[HBM] * 7,
            out_specs=VMEM,
            scratch_shapes=raw_scratch,
            compiler_params=pltpu.CompilerParams(vmem_limit_bytes=63 * 1024 * 1024),
        )(*operands)
        got = lax.all_to_all(packed, "tile", split_axis=0, concat_axis=0, tiled=True)
        places = got.reshape(slots, TILES, 16, TS)[:, TILES - 1, 6, 0].astype(jnp.int32)
        columns = pl.pallas_call(
            full_grid_kernel,
            out_shape=columns_shape,
            in_specs=[SMEM, VMEM, HBM],
            out_specs=VMEM,
            scratch_shapes=grid_scratch,
            compiler_params=PARAMS,
        )(places, got, v_table)
        return plain_image(columns)

    held = pl.pallas_call(
        hold_kernel,
        out_shape=[jax.ShapeDtypeStruct((2 * TS, IMX), jnp.bfloat16)] * HELD
        + [jax.ShapeDtypeStruct((2 * TS, IMX), jnp.bfloat16)],
        in_specs=[SMEM, HBM],
        out_specs=[VMEM] * (HELD + 1),
        scratch_shapes=[pltpu.SemaphoreType.DMA((HELD + 2 * PEERS,))],
        compiler_params=PARAMS,
        cost_estimate=pl.CostEstimate(flops=0, bytes_accessed=16 * 10 ** 6, transcendentals=0),
    )(flags, u_table)
    image = pl.pallas_call(
        functools.partial(image_kernel, scale),
        out_shape=image_shape,
        in_specs=[VMEM] * (HELD + 2) + [HBM],
        out_specs=VMEM,
        scratch_shapes=[
            pltpu.VMEM(((bands - HELD) * 2 * TS, IMX), jnp.bfloat16),
            pltpu.SemaphoreType.DMA((bands - HELD,)),
        ],
        compiler_params=PARAMS,
    )(exchanged(columns), *held, u_table)
    return lax.cond(flags[0] == 1, lambda kept: kept, every_slot, image)


def solution(mesh):
    placed = (
        P("chan", None, "tile"),
        P("chan", None, "tile"),
        P("chan", None, "tile"),
        P("tile"),
        P("tile"),
        P("tile", None),
        P("tile"),
    )
    return jax.shard_map(
        body, mesh=mesh, in_specs=placed, out_specs=P(("tile", "chan"), None), check_vma=False
    )
```

```python
import functools
import math

import jax
import jax.numpy as jnp
import ml_dtypes
import numpy as np
from jax import lax
from jax.experimental import pallas as pl
from jax.experimental.pallas import tpu as pltpu
from jax.sharding import PartitionSpec as P

NG = 16384
CH = 4
KS = 8
BLOCK = 256
TS = 128
TPD = 8
NB = 32
IMX = 1024
IMY = 1024
ROWS = 80
TILES = ROWS // 16
DIRECT = 2
HELD = 4
PEERS = 4
MANY = 255


def phase_table(rows_coord, cols_coord):
    turns = np.mod(rows_coord[:, None].astype(np.int64) * cols_coord[None, :].astype(np.int64), NG)
    angles = turns.astype(np.float64) * (2.0 * math.pi / NG)
    return np.cos(angles).astype(ml_dtypes.bfloat16), np.sin(angles).astype(ml_dtypes.bfloat16)


def column_table():
    cos_v, sin_v = phase_table(np.arange(IMY) - IMY // 2, np.arange(TPD * TS))
    return np.concatenate([cos_v, sin_v], axis=1)


def image_table(bands):
    cos_u, sin_u = phase_table(np.arange(bands * TS), np.arange(IMX) - IMX // 2)
    both = np.stack([cos_u.reshape(bands, TS, IMX), (-sin_u).reshape(bands, TS, IMX)], axis=1)
    return both.reshape(bands * 2 * TS, IMX)


def full_pack_kernel(
    capacity,
    route_hbm, slot_hbm, u_hbm, v_hbm, vis_hbm, uo_hbm, vo_hbm, out_ref,
    route, slot, u_ref, v_ref, vis_ref, uo_ref, vo_ref, count, sems,
):
    copies = start_all(
        (
            (route_hbm, route), (slot_hbm, slot), (u_hbm, u_ref), (v_hbm, v_ref),
            (vis_hbm, vis_ref), (uo_hbm, uo_ref), (vo_hbm, vo_ref),
        ),
        sems,
    )
    for copy in copies:
        copy.wait()
    owners = out_ref.shape[0] // (capacity * TILES)
    out_ref[...] = jnp.zeros_like(out_ref)

    def clear(owner, _):
        count[owner] = 0
        return 0

    lax.fori_loop(0, owners, clear, 0)
    for block in range(NB):
        owner = route[block]
        rank = count[owner]
        count[owner] = rank + 1
        base = (owner * capacity + rank) * TILES
        place = jnp.full((1, TS), slot[block] + 1, jnp.int32).astype(jnp.float32)
        misc = []
        for half in range(2):
            lanes = slice(block * BLOCK + half * TS, block * BLOCK + half * TS + TS)
            row = block * 2 + half
            out_ref[base + half] = u_ref[:, lanes]
            out_ref[base + 2 + half] = v_ref[:, lanes]
            misc += [
                vis_ref[0, :, lanes].astype(jnp.float32),
                vis_ref[1, :, lanes].astype(jnp.float32),
                uo_ref[row:row + 1, :].astype(jnp.float32),
                vo_ref[row:row + 1, :].astype(jnp.float32),
                place,
                jnp.zeros((1, TS), jnp.float32),
            ]
        out_ref[base + 4] = jnp.concatenate(misc, axis=0).astype(jnp.bfloat16)


def turned(kernel, first):
    for bit in (1, 2, 4):
        kernel = jnp.where((first & bit) != 0, pltpu.roll(kernel, bit, 0), kernel)
    return kernel


def spread(kernel, first_tile):
    both = jnp.concatenate([kernel, kernel], axis=0).astype(jnp.bfloat16)
    zero = jnp.zeros_like(both)
    return jnp.concatenate(
        [jnp.where(first_tile == pair * 2, both, zero) for pair in range(TS // 16)], axis=0
    )


def tile_of(first):
    sub = lax.broadcasted_iota(jnp.int32, (8, TS), 0)
    tile = lax.shift_right_logical(first + ((sub - first) & 7), 3)
    return jnp.concatenate([tile, tile - 1], axis=0).astype(jnp.float32).astype(jnp.bfloat16)


def block_tile(halves):
    v_parts, w_parts = [], []
    for u_two, v_two, own in halves:
        u_first = jnp.broadcast_to(own[4:5], (8, TS)).astype(jnp.int32)
        v_first = jnp.broadcast_to(own[5:6], (8, TS)).astype(jnp.int32)
        u_tile, v_tile = tile_of(u_first), tile_of(v_first)
        for chan in range(2):
            v_parts.append(spread(turned(v_two[8 * chan:8 * chan + 8], v_first), v_tile))
            u_turned = turned(u_two[8 * chan:8 * chan + 8], u_first)
            w_parts.append(jnp.concatenate(
                [spread(u_turned * own[2 * chan + part:2 * chan + part + 1], u_tile) for part in range(2)],
                axis=0,
            ))
    return dot_rows(jnp.concatenate(w_parts, axis=1), jnp.concatenate(v_parts, axis=1))


def dot_rows(left, right):
    return lax.dot_general(left, right, (((1,), (1,)), ((), ())), preferred_element_type=jnp.float32)


def start_all(pairs, sems):
    copies = [pltpu.make_async_copy(source, target, sems.at[turn]) for turn, (source, target) in enumerate(pairs)]
    for copy in copies:
        copy.start()
    return copies


def clear_counts(count, bands):
    def clear(owner, _):
        count[owner] = 0
        return 0

    lax.fori_loop(0, bands, clear, 0)


def overflow_mark(route, count):
    mark = jnp.int32(0)
    for block in range(NB):
        owner = route[block]
        seen = count[owner]
        count[owner] = seen + 1
        mark = jnp.where(seen == DIRECT, jnp.where(mark == 0, owner + 1, MANY), mark)
    return mark


def pack_kernel(
    bands, shared,
    route_hbm, slot_hbm, u_hbm, v_hbm, vis_hbm, uo_hbm, vo_hbm, out_ref,
    route, slot, u_ref, v_ref, vis_ref, uo_ref, vo_ref, count, sems,
):
    copies = start_all(
        (
            (route_hbm, route), (slot_hbm, slot), (u_hbm, u_ref), (v_hbm, v_ref),
            (vis_hbm, vis_ref), (uo_hbm, uo_ref), (vo_hbm, vo_ref),
        ),
        sems,
    )
    per_owner = DIRECT * TILES
    clear_counts(count, bands)
    copies[0].wait()
    copies[1].wait()
    mark = jnp.int32(0)
    if shared:
        mark = overflow_mark(route, count)
        clear_counts(count, bands)
    marks = jnp.broadcast_to(mark, (1, TS)).astype(jnp.float32)
    nothing = jnp.zeros((7, TS), jnp.float32)
    blank = jnp.concatenate([nothing, marks, nothing, marks], axis=0).astype(jnp.bfloat16)
    empty = jnp.zeros((16, TS), jnp.bfloat16)
    for target in range(bands * DIRECT):
        for tile in range(TILES - 1):
            out_ref[target * TILES + tile] = empty
        out_ref[target * TILES + TILES - 1] = blank
    for copy in copies[2:]:
        copy.wait()

    for block in range(NB):
        owner = route[block]
        rank = count[owner]
        count[owner] = rank + 1
        base = owner * per_owner + rank * TILES

        @pl.when((owner + 1 != mark) & (rank < DIRECT))
        def _():
            place = jnp.full((1, TS), slot[block] + 1, jnp.int32).astype(jnp.float32)
            misc = []
            for half in range(2):
                lanes = slice(block * BLOCK + half * TS, block * BLOCK + half * TS + TS)
                row = block * 2 + half
                out_ref[base + half] = u_ref[:, lanes]
                out_ref[base + 2 + half] = v_ref[:, lanes]
                misc += [
                    vis_ref[0, :, lanes].astype(jnp.float32),
                    vis_ref[1, :, lanes].astype(jnp.float32),
                    uo_ref[row:row + 1, :].astype(jnp.float32),
                    vo_ref[row:row + 1, :].astype(jnp.float32),
                    place,
                    marks,
                ]
            out_ref[base + 4] = jnp.concatenate(misc, axis=0).astype(jnp.bfloat16)


def own_kernel(
    bands,
    route_hbm, slot_hbm, u_hbm, v_hbm, vis_hbm, uo_hbm, vo_hbm, table_hbm, share_0, share_1, share_2, share_3,
    route, slot, u_ref, v_ref, vis_ref, uo_ref, vo_ref, count, sems, listed, grid, table, table_sem,
):
    copies = start_all(
        (
            (route_hbm, route), (slot_hbm, slot), (u_hbm, u_ref), (v_hbm, v_ref),
            (vis_hbm, vis_ref), (uo_hbm, uo_ref), (vo_hbm, vo_ref),
        ),
        sems,
    )
    table_copy = pltpu.make_async_copy(table_hbm, table, table_sem)
    table_copy.start()
    grid[...] = jnp.zeros_like(grid)
    clear_counts(count, bands)
    copies[0].wait()
    copies[1].wait()
    mark = overflow_mark(route, count)
    filled = jnp.int32(0)
    for block in range(NB):
        listed[filled] = block
        filled = filled + (route[block] + 1 == mark).astype(jnp.int32)
    for copy in copies[2:]:
        copy.wait()

    def own_tile(block, used):
        halves = []
        for half in range(2):
            lanes = pl.ds(pl.multiple_of(block * BLOCK + half * TS, TS), TS)
            row = pl.ds(block * 2 + half, 1)
            own = jnp.concatenate(
                [
                    vis_ref[0, :, lanes].astype(jnp.float32) * used,
                    vis_ref[1, :, lanes].astype(jnp.float32) * used,
                    uo_ref[row, :].astype(jnp.float32),
                    vo_ref[row, :].astype(jnp.float32),
                ],
                axis=0,
            )
            halves.append((u_ref[:, lanes].astype(jnp.float32), v_ref[:, lanes].astype(jnp.float32), own))
        return block_tile(halves)

    def add_blocks(turn, _):
        for lane in range(4):
            number = turn * 4 + lane
            block = listed[jnp.minimum(number, filled - 1)]
            cells = pl.ds(pl.multiple_of(slot[block] * TS, TS), TS)
            grid[:, cells] += own_tile(block, (number < filled).astype(jnp.float32))
        return 0

    lax.fori_loop(0, (filled + 3) // 4, add_blocks, 0)
    me = lax.axis_index("tile") % PEERS
    width = TS // PEERS
    shares = (share_0, share_1, share_2, share_3)
    plain, turned_over = [], []
    for turn in range(PEERS):
        first = pl.multiple_of((me ^ turn) * width, width)
        real, imag = [grid[pl.ds(part * TS + first, width), :].astype(jnp.bfloat16) for part in range(2)]
        plain += [real, imag]
        turned_over += [-imag, real]
    both = jnp.concatenate([jnp.concatenate(plain, axis=0), jnp.concatenate(turned_over, axis=0)], axis=1)
    rows = IMY // share_0.shape[0]
    step = 256
    table_copy.wait()
    for first in range(0, IMY, step):
        part = dot_rows(table[first:first + step, :], both).astype(jnp.bfloat16)
        for row in range(0, step, rows):
            middle = row + rows // 2
            for turn, share_ref in enumerate(shares):
                lanes = slice(2 * width * turn, 2 * width * (turn + 1))
                pieces = [part[row:middle, lanes], part[middle:row + rows, lanes]]
                share_ref[(first + row) // rows] = jnp.concatenate(pieces, axis=1)


def hold_kernel(flags, table_hbm, *refs):
    parts, own, sems = refs[:-2], refs[-2], refs[-1]
    rows = parts[0].shape[0]
    pairs = [(table_hbm.at[pl.ds(turn * rows, rows), :], part) for turn, part in enumerate(parts)]
    width = TS // PEERS
    for turn in range(2 * PEERS):
        peer, part = turn // 2, turn % 2
        first = pl.multiple_of((flags[1] * 2 + part) * TS + peer * width, width)
        pairs.append((table_hbm.at[pl.ds(first, width), :], own.at[pl.ds(turn * width, width), :]))
    for copy in start_all(pairs, sems):
        copy.wait()


def got_tile(got_ref, base):
    misc = got_ref[base + 4].astype(jnp.float32)
    halves = [
        (got_ref[base + half].astype(jnp.float32), got_ref[base + 2 + half].astype(jnp.float32), misc[8 * half:8 * half + 8])
        for half in range(2)
    ]
    return misc, block_tile(halves)


def turned_parts(rounded):
    half = rounded.shape[0] // 2
    return jnp.concatenate([rounded, jnp.concatenate([-rounded[half:], rounded[:half]], axis=0)], axis=1)


def write_columns(grid, table, out_ref):
    both = turned_parts(grid[...].astype(jnp.bfloat16))
    rows = IMY // out_ref.shape[0]
    step = 256
    for first in range(0, IMY, step):
        part = dot_rows(table[first:first + step, :], both)
        for row in range(0, step, rows):
            pieces = [part[row:row + rows, :TS], part[row:row + rows, TS:]]
            out_ref[(first + row) // rows, :2 * rows, :] = jnp.concatenate(pieces, axis=0).astype(jnp.bfloat16)


def full_grid_kernel(places, got_ref, table_hbm, out_ref, grid, table, sem):
    copy = pltpu.make_async_copy(table_hbm, table, sem)
    copy.start()
    grid[...] = jnp.zeros_like(grid)
    tiles = got_ref.shape[0]

    def add_slot(index, _):
        @pl.when(places[index] > 0)
        def _():
            cells = pl.ds(pl.multiple_of((places[index] - 1) * TS, TS), TS)
            grid[:, cells] += got_tile(got_ref, index * TILES)[1]

        return 0

    lax.fori_loop(0, tiles // TILES, add_slot, 0)
    out_ref[...] = jnp.zeros_like(out_ref)
    copy.wait()
    write_columns(grid, table, out_ref)


def grid_kernel(bands, shared, got_ref, *refs):
    shares = refs[:PEERS] if shared else ()
    table_hbm, out_ref, flags, grid, table, sem = refs[len(shares):]
    copy = pltpu.make_async_copy(table_hbm, table, sem)
    copy.start()
    grid[...] = jnp.zeros_like(grid)
    per_owner = DIRECT * TILES

    def add_source(source, carried):
        least, most = carried
        for rank in range(DIRECT):
            misc, tile = got_tile(got_ref, source * per_owner + rank * TILES)
            place = jnp.maximum(misc[6, 0].astype(jnp.int32) - 1, 0)
            cells = pl.ds(pl.multiple_of(place * TS, TS), TS)
            grid[:, cells] += tile
        marks = misc[:8]
        return jnp.minimum(least, jnp.where(marks == 0.0, float(MANY), marks)), jnp.maximum(most, marks)

    start = (jnp.full((8, TS), float(MANY), jnp.float32), jnp.zeros((8, TS), jnp.float32))
    least, most = lax.fori_loop(0, bands, add_source, start, unroll=8)
    low, high = least[7, 0].astype(jnp.int32), most[7, 0].astype(jnp.int32)
    flags[0] = ((high == 0) | ((low == high) & (high != MANY))).astype(jnp.int32)
    flags[1] = jnp.where(high == MANY, 0, jnp.maximum(high - 1, 0))
    if shared:
        own = shares[0][...].astype(jnp.float32)
        for share in shares[1:]:
            own += share[...].astype(jnp.float32)
        out_ref[:, out_ref.shape[1] - 16:, :] = own.astype(jnp.bfloat16)
    copy.wait()
    write_columns(grid, table, out_ref)


def side_by_side(got_ref, band, group, first, rows):
    return jnp.concatenate(
        [got_ref[band, group, first:first + rows, :], got_ref[band, group, first + rows:first + 2 * rows, :]], axis=1
    )


def band_dot(got_ref, table, rows, bands):
    left = jnp.concatenate(
        [
            jnp.concatenate([side_by_side(got_ref, band, group, 0, rows) for band in bands], axis=1)
            for group in range(got_ref.shape[1])
        ],
        axis=0,
    )
    return jnp.dot(left, table, preferred_element_type=jnp.float32)


def image_kernel(scale, got_ref, *refs):
    held = refs[:HELD]
    own_ref, table_hbm, out_ref, table_ref, sems = refs[HELD:]
    rows = out_ref.shape[0]
    bands, groups = got_ref.shape[:2]
    pairs = []
    for band in range(HELD, bands):
        lines = pl.ds(band * 2 * TS, 2 * TS)
        pairs.append((table_hbm.at[lines, :], table_ref.at[pl.ds((band - HELD) * 2 * TS, 2 * TS), :]))
    copies = start_all(pairs, sems)
    width = TS // PEERS
    left = []
    for peer in range(PEERS):
        per_group = []
        for group in range(groups):
            added = got_ref[peer, group, 2 * rows:, :].astype(jnp.float32)
            for band in range(peer + PEERS, bands, PEERS):
                added += got_ref[band, group, 2 * rows:, :].astype(jnp.float32)
            per_group += [added[:, :2 * width], added[:, 2 * width:]]
        left.append(jnp.concatenate(per_group, axis=0))
    total = jnp.dot(
        jnp.concatenate(left, axis=1).astype(jnp.bfloat16), own_ref[...], preferred_element_type=jnp.float32
    )
    table = jnp.concatenate([part[...] for part in held], axis=0)
    total = total + band_dot(got_ref, table, rows, range(HELD))
    for first in range(HELD, bands, HELD):
        for band in range(first, first + HELD):
            copies[band - HELD].wait()
        table = table_ref[(first - HELD) * 2 * TS:first * 2 * TS, :]
        total = total + band_dot(got_ref, table, rows, range(first, first + HELD))
    image = total[:rows]
    for group in range(1, groups):
        image = image + total[group * rows:(group + 1) * rows]
    out_ref[...] = image * scale


def plain_image_kernel(scale, got_ref, table_ref, out_ref, total):
    turn = pl.program_id(0)

    @pl.when(turn == 0)
    def _():
        total[...] = jnp.zeros_like(total)

    rows = out_ref.shape[0]
    part = total[...] + band_dot(got_ref, table_ref[...], rows, range(got_ref.shape[0]))
    total[...] = part

    @pl.when(turn == pl.num_programs(0) - 1)
    def _():
        out_ref[...] = (part[:rows] + part[rows:]) * scale


VMEM = pl.BlockSpec(memory_space=pltpu.VMEM)
SMEM = pl.BlockSpec(memory_space=pltpu.SMEM)
HBM = pl.BlockSpec(memory_space=pltpu.HBM)
PARAMS = pltpu.CompilerParams(vmem_limit_bytes=20 * 1024 * 1024)


def body(visibility, u_kernel, v_kernel, u_offset, v_offset, tile_route, tile_slot):
    bands = lax.axis_size("tile")
    groups = lax.axis_size("chan")
    local_rows = visibility.shape[2]
    capacity = 4 * NB // bands
    shared = capacity > DIRECT
    rows_y = IMY // (bands * groups)
    sent_rows = 2 * rows_y + (16 if shared else 0)
    columns_shape = jax.ShapeDtypeStruct((bands * groups, sent_rows, TS), jnp.bfloat16)
    v_table = jnp.asarray(column_table())
    operands = (
        tile_route[:, 0],
        tile_slot,
        u_kernel.reshape(2 * KS, local_rows),
        v_kernel.reshape(2 * KS, local_rows),
        visibility,
        u_offset.reshape(NB * 2, TS),
        v_offset.reshape(NB * 2, TS),
    )
    grid_scratch = [
        pltpu.VMEM((2 * TS, TPD * TS), jnp.float32),
        pltpu.VMEM((IMY, 2 * TPD * TS), jnp.bfloat16),
        pltpu.SemaphoreType.DMA,
    ]
    raw_scratch = [
        pltpu.SMEM((NB,), jnp.int32),
        pltpu.SMEM((NB,), jnp.int32),
        pltpu.VMEM((2 * KS, local_rows), jnp.bfloat16),
        pltpu.VMEM((2 * KS, local_rows), jnp.bfloat16),
        pltpu.VMEM(visibility.shape, jnp.bfloat16),
        pltpu.VMEM((NB * 2, TS), jnp.int32),
        pltpu.VMEM((NB * 2, TS), jnp.int32),
    ]
    raw_scratch += [pltpu.SMEM((bands,), jnp.int32), pltpu.SemaphoreType.DMA((7,))]
    packed = pl.pallas_call(
        functools.partial(pack_kernel, bands, shared),
        out_shape=jax.ShapeDtypeStruct((bands * DIRECT * TILES, 16, TS), jnp.bfloat16),
        in_specs=[HBM] * 7,
        out_specs=VMEM,
        scratch_shapes=raw_scratch,
        compiler_params=PARAMS,
    )(*operands)
    got = lax.all_to_all(packed, "tile", split_axis=0, concat_axis=0, tiled=True)
    u_table = jnp.asarray(image_table(bands))
    partial = ()
    if shared:
        own = pl.pallas_call(
            functools.partial(own_kernel, bands),
            out_shape=[jax.ShapeDtypeStruct((bands * groups, 16, TS), jnp.bfloat16)] * PEERS,
            in_specs=[HBM] * 8,
            out_specs=[VMEM] * PEERS,
            scratch_shapes=raw_scratch + [
                pltpu.SMEM((NB + 1,), jnp.int32), pltpu.VMEM((2 * TS, TPD * TS), jnp.float32),
                pltpu.VMEM((IMY, 2 * TPD * TS), jnp.bfloat16), pltpu.SemaphoreType.DMA,
            ],
            compiler_params=PARAMS,
            cost_estimate=pl.CostEstimate(flops=10 ** 9, bytes_accessed=6 * 10 ** 6, transcendentals=0),
        )(*operands, v_table)
        summed = [own[0]] + [
            lax.ppermute(own[turn], "tile", [(band, band ^ turn) for band in range(bands)]) for turn in (3, 2, 1)
        ]
        partial = tuple(summed)
    columns, flags = pl.pallas_call(
        functools.partial(grid_kernel, bands, shared),
        out_shape=(columns_shape, jax.ShapeDtypeStruct((2,), jnp.int32)),
        in_specs=[VMEM] * (1 + len(partial)) + [HBM],
        out_specs=(VMEM, SMEM),
        scratch_shapes=grid_scratch,
        compiler_params=PARAMS,
    )(got, *partial, v_table)

    scale = 1.0 / (KS * KS * math.sqrt(local_rows * bands * CH))
    image_shape = jax.ShapeDtypeStruct((rows_y, IMX), jnp.float32)

    def exchanged(columns):
        sent = lax.all_to_all(columns, ("tile", "chan"), split_axis=0, concat_axis=0, tiled=True)
        return sent.reshape(bands, groups, sent_rows, TS)

    def plain_image(columns):
        per_turn = 4
        return pl.pallas_call(
            functools.partial(plain_image_kernel, scale),
            out_shape=image_shape,
            grid=(bands // per_turn,),
            in_specs=[
                pl.BlockSpec((per_turn, groups, sent_rows, TS), lambda turn: (turn, 0, 0, 0)),
                pl.BlockSpec((per_turn * 2 * TS, IMX), lambda turn: (turn, 0)),
            ],
            out_specs=pl.BlockSpec((rows_y, IMX), lambda turn: (0, 0)),
            scratch_shapes=[pltpu.VMEM((groups * rows_y, IMX), jnp.float32)],
            compiler_params=PARAMS,
        )(exchanged(columns), u_table)

    if not shared:
        return plain_image(columns)

    def every_slot(_):
        slots = bands * capacity
        packed = pl.pallas_call(
            functools.partial(full_pack_kernel, capacity),
            out_shape=jax.ShapeDtypeStruct((slots * TILES, 16, TS), jnp.bfloat16),
            in_specs=[HBM] * 7,
            out_specs=VMEM,
            scratch_shapes=raw_scratch,
            compiler_params=pltpu.CompilerParams(vmem_limit_bytes=63 * 1024 * 1024),
        )(*operands)
        got = lax.all_to_all(packed, "tile", split_axis=0, concat_axis=0, tiled=True)
        places = got.reshape(slots, TILES, 16, TS)[:, TILES - 1, 6, 0].astype(jnp.int32)
        columns = pl.pallas_call(
            full_grid_kernel,
            out_shape=columns_shape,
            in_specs=[SMEM, VMEM, HBM],
            out_specs=VMEM,
            scratch_shapes=grid_scratch,
            compiler_params=PARAMS,
        )(places, got, v_table)
        return plain_image(columns)

    held = pl.pallas_call(
        hold_kernel,
        out_shape=[jax.ShapeDtypeStruct((2 * TS, IMX), jnp.bfloat16)] * HELD
        + [jax.ShapeDtypeStruct((2 * TS, IMX), jnp.bfloat16)],
        in_specs=[SMEM, HBM],
        out_specs=[VMEM] * (HELD + 1),
        scratch_shapes=[pltpu.SemaphoreType.DMA((HELD + 2 * PEERS,))],
        compiler_params=PARAMS,
        cost_estimate=pl.CostEstimate(flops=0, bytes_accessed=16 * 10 ** 6, transcendentals=0),
    )(flags, u_table)
    image = pl.pallas_call(
        functools.partial(image_kernel, scale),
        out_shape=image_shape,
        in_specs=[VMEM] * (HELD + 2) + [HBM],
        out_specs=VMEM,
        scratch_shapes=[
            pltpu.VMEM(((bands - HELD) * 2 * TS, IMX), jnp.bfloat16),
            pltpu.SemaphoreType.DMA((bands - HELD,)),
        ],
        compiler_params=PARAMS,
    )(exchanged(columns), *held, u_table)
    return lax.cond(flags[0] == 1, lambda kept: kept, every_slot, image)


def solution(mesh):
    placed = (
        P("chan", None, "tile"),
        P("chan", None, "tile"),
        P("chan", None, "tile"),
        P("tile"),
        P("tile"),
        P("tile", None),
        P("tile"),
    )
    return jax.shard_map(
        body, mesh=mesh, in_specs=placed, out_specs=P(("tile", "chan"), None), check_vma=False
    )
```
